32 devices in a mesh: ka: 16 (over z, y, x), ga: 2 (over core).
Axes of the slice: x: 2, y: 2, z: 4, core: 2. Of those that a mesh axis runs over, the one named last changes fastest.
Arguments:
- densities: bfloat16 [64, 6144, 128], P('ka'), may hold values from -0.67578125 to 0.67578125
- screened: bfloat16 [2, 6144, 6144], P(None, 'ka', 'ga'), may hold values from -0.0546875 to 0.0546875
- partner: int32 [64], replicated, may hold values from 0 to 63, as said below
- pair_order: int32 [64], replicated, may hold values from 0 to 63, each once
Outputs:
- direct: float32 [64, 64, 128], P('ka')
- mirror: float32 [64, 64, 128], P('ka')
The draws below stay inside these ranges and needn't reach their ends.
Inputs may be any that keep to these rules, and one draw needn't show every extreme that they name: Number the k-points of a 4 x 4 x 4 grid as k = (a * 4 + b) * 4 + c. partner[k] is the k-point (a + 1, b, c + s) with wrap-around in each direction, for one s from 0 to 3 drawn with the seed.
All inputs are finite; a program needn't handle non-finite values.
Results may differ from the reference program's by a relative error of at most 0.0003.
Values may be sent and summed in bfloat16 or wider, within the bound.
No kernel may reach another device: no remote copies, remote signals or barrier semaphores. Data moves between devices by JAX's collectives and lax.ppermute only.
A program may use at most 192 MiB of HBM per device.

```python
import jax
import jax.numpy as jnp
from jax import lax

NG = 6144
NP = 64
K_DEV = 4
NK = 64
KGX = 4


def draw_partner(key, part):
    key = jax.random.fold_in(key, 11)
    slot_shift = jax.random.randint(key, (), 0, K_DEV)
    number = jnp.arange(NK, dtype=jnp.int32)
    inner = number % K_DEV
    middle = number // K_DEV % 4
    outer = number // (4 * K_DEV)
    return (((outer + 1) % KGX * 4 + middle) * K_DEV + (inner + slot_shift) % K_DEV).astype(jnp.int32)


def shard_levels(rng, extent, shards, least, top_value):
    factor_of = 1.0
    for dim, blocks in shards:
        heights = jax.random.uniform(jax.random.fold_in(jax.random.fold_in(rng, 6), dim), (blocks,), jnp.float32, least / len(shards), top_value / len(shards))
        factor_of = factor_of * jnp.repeat(jnp.exp(heights), extent[dim] // blocks).reshape((-1,) + (1,) * (len(extent) - 1 - dim))
    return factor_of


def centred(stream_key, shape, deviation, most, shards=(), held_as=jnp.bfloat16):
    drawn = deviation * jax.random.normal(stream_key, shape, jnp.float32)
    if shards:
        drawn = drawn * shard_levels(stream_key, shape, shards, -0.22, 0.18)
    return jnp.clip(drawn, -most, most).astype(held_as)


def setup_inputs(seed: int = 0) -> dict:
    streams_of = jax.random.split(jax.random.key(seed), 5)
    return {
        "densities": centred(streams_of[0], (NK, NG, 2 * NP), (NG ** -0.25), 0.67578125, ((0, 16),)),
        "screened": centred(streams_of[1], (2, NG, NG), (2 * NG) ** -0.5, 0.0546875, ((1, 16), (2, 2))),
        "partner": draw_partner(jax.random.fold_in(streams_of[4], 71), 0),
        "pair_order": jax.random.permutation(streams_of[3], NP).astype(jnp.int32),
    }


def reference(densities, screened, partner, pair_order):
    flipped = jnp.transpose(densities, (0, 2, 1)).reshape(NK * 2 * NP, NG)
    real_side = jnp.dot(flipped, screened[0], preferred_element_type=jnp.float32).reshape(NK, 2 * NP, NG)
    imag_side = jnp.dot(flipped, screened[1], preferred_element_type=jnp.float32).reshape(NK, 2 * NP, NG)
    left_re = real_side[:, :NP] + imag_side[:, NP:]
    left_im = imag_side[:, :NP] - real_side[:, NP:]
    left_factor = jnp.stack([left_re, left_im], axis=1)
    matched = jnp.take(densities, partner, axis=0)
    partial_value = jnp.einsum("kwpg,kgq->kwpq", left_factor, matched.astype(jnp.float32),
                         precision=lax.Precision.HIGHEST)
    block_re = partial_value[:, 0, :, :NP] - partial_value[:, 1, :, NP:]
    block_im = partial_value[:, 0, :, NP:] + partial_value[:, 1, :, :NP]
    block_re = jnp.take(block_re, pair_order, axis=2)
    block_im = jnp.take(block_im, pair_order, axis=2)
    direct = jnp.concatenate([block_re, block_im], axis=2)
    flipped_back = jnp.concatenate([jnp.swapaxes(block_re, 1, 2), -jnp.swapaxes(block_im, 1, 2)], axis=2)
    mirror = jnp.zeros_like(direct).at[partner].set(flipped_back)
    return (direct, mirror)
```

```python
import functools

import jax
import jax.numpy as jnp
from jax import lax
from jax.experimental import pallas as pl
from jax.experimental.pallas import tpu as pltpu
from jax.sharding import PartitionSpec as P


def passed_along(value, axis, steps):
    count = lax.axis_size(axis)
    pairs = [(source, (source + steps) % count) for source in range(count)]
    return lax.ppermute(value, axis, pairs)


def conjugate_side(blocks, pair_count):
    real_half = jnp.swapaxes(blocks[:, :, :pair_count], 1, 2)
    imag_half = jnp.swapaxes(blocks[:, :, pair_count:], 1, 2)
    return jnp.concatenate([real_half, -imag_half], axis=2)


def combine_terms(partial_value, order_table, pair_count):
    block_re = partial_value[:, 0, :, :pair_count] - partial_value[:, 1, :, pair_count:]
    block_im = partial_value[:, 0, :, pair_count:] + partial_value[:, 1, :, :pair_count]
    return reorder(block_re, block_im, order_table)


def reorder(block_re, block_im, order_table):
    block_re = jnp.einsum("kpq,qj->kpj", block_re, order_table, precision=lax.Precision.HIGHEST)
    block_im = jnp.einsum("kpq,qj->kpj", block_im, order_table, precision=lax.Precision.HIGHEST)
    return jnp.concatenate([block_re, block_im], axis=2)


def finish_terms(left_sums, matched, pair_count):
    left_re = left_sums[:, 0, :pair_count] + left_sums[:, 1, pair_count:]
    left_im = left_sums[:, 1, :pair_count] - left_sums[:, 0, pair_count:]
    left_factor = jnp.stack([left_re, left_im], axis=1)
    return jnp.einsum(
        "kwpc,kcq->kwpq", left_factor, matched.astype(jnp.float32), precision=lax.Precision.HIGHEST
    )


def general_body(densities, screened, partner, pair_order):
    k_count = densities.shape[0]
    pair_count = densities.shape[2] // 2
    panel_width = screened.shape[2]
    k_owner = lax.axis_index("ka")
    column = lax.axis_index("ga")
    own_columns = lax.dynamic_slice_in_dim(densities, column * panel_width, panel_width, 1)
    arrived = passed_along(own_columns, "ka", -4)
    own_partner = lax.dynamic_slice_in_dim(partner, k_owner * k_count, k_count, 0)
    slot_index = own_partner % k_count
    offset = slot_index[0]
    matched = jnp.take(arrived, slot_index, axis=0)
    left_sums = jnp.einsum(
        "kgp,wgc->kwpc",
        densities,
        lax.all_gather(screened, "ka", axis=1, tiled=True),
        preferred_element_type=jnp.float32,
    )
    partial_value = finish_terms(left_sums, matched, pair_count)
    order_table = (jnp.arange(pair_count)[:, None] == pair_order[None, :]).astype(jnp.float32)
    sources = (jnp.arange(k_count) - offset) % k_count
    summed = lax.psum(partial_value, "ga")
    direct = combine_terms(summed, order_table, pair_count)
    received = passed_along(direct, "ka", 4)
    mirror = conjugate_side(jnp.take(received, sources, axis=0), pair_count)
    return (direct, mirror)


AXES = ("ka", "ga")
CHUNKS = 3


def device(z, b, c):
    return (z * 4 + b) * 2 + c


def moved(value, rule):
    pairs = []
    for z in range(4):
        for b in range(4):
            for c in range(2):
                target = rule(z, b, c)
                if target is not None:
                    pairs.append((device(z, b, c), device(*target)))
    return lax.ppermute(value, AXES, pairs)


def along_x(value):
    return moved(value, lambda z, b, c: (z, b ^ 1, c))


def along_y(value):
    return moved(value, lambda z, b, c: (z, b ^ 2, c))


def other_core(value):
    return moved(value, lambda z, b, c: (z, b, 1 - c))


def end_with_mid(value):
    return moved(value, lambda z, b, c: (z ^ 1, b, c))


def mid_to_end(value):
    return moved(value, lambda z, b, c: (z ^ 1, b, c) if z in (1, 2) else None)


def mid_with_mid(value):
    return moved(value, lambda z, b, c: (3 - z, b, c) if z in (1, 2) else None)


def in_plane(chunk):
    x_side = along_x(chunk)
    y_side = along_y(chunk)
    diagonal_re = along_y(x_side[0])
    diagonal_im = along_x(y_side[1])
    return (chunk, x_side, y_side, diagonal_re, diagonal_im)


def terms_kernel(flags, *refs, n_chunks, slots, near):
    n_slots = len(slots)
    w_refs = [refs[5 * i : 5 * i + 5] for i in range(n_chunks)]
    rest = refs[5 * n_chunks :]
    carried, swapped = rest[:n_slots], rest[n_slots : 2 * n_slots]
    up_refs, down_refs = rest[2 * n_slots : 3 * n_slots], rest[3 * n_slots : 4 * n_slots]
    rest = rest[4 * n_slots :]
    acc_in, acc, w_buf, m_buf, c_buf, w_sems, m_sems, c_sems = rest
    own_b, own_near, half, shift = flags[0], flags[1], flags[2], flags[3]
    rows = w_refs[0][0].shape[1]
    width = w_refs[0][0].shape[2]
    depth = 4 * rows
    copies = []
    for i in range(n_chunks):
        own, x_side, y_side, d_re, d_im = w_refs[i]
        here = []
        for turn, source in ((0, own), (1, x_side), (2, y_side)):
            start = pl.multiple_of((own_b ^ turn) * rows, rows)
            here.append(pltpu.make_async_copy(source, w_buf.at[i, :, pl.ds(start, rows), :], w_sems.at[i, turn]))
        start = pl.multiple_of((own_b ^ 3) * rows, rows)
        for part, source in ((0, d_re), (1, d_im)):
            here.append(pltpu.make_async_copy(source, w_buf.at[i, part, pl.ds(start, rows), :], w_sems.at[i, 3 + part]))
        copies.append(here)
    chosen = own_near == (1 if near else 0)
    for copy in copies[0]:
        copy.start()
    m_waits, c_waits = [], []
    for s in range(n_slots):
        first = pltpu.make_async_copy(carried[s], m_buf.at[s], m_sems.at[s])
        second = pltpu.make_async_copy(swapped[s], m_buf.at[s], m_sems.at[s])
        pl.when(chosen)(first.start)
        pl.when(jnp.logical_not(chosen))(second.start)
        m_waits.append(first)
        first = pltpu.make_async_copy(up_refs[s], c_buf.at[s], c_sems.at[s])
        second = pltpu.make_async_copy(down_refs[s], c_buf.at[s], c_sems.at[s])
        pl.when(half == 0)(first.start)
        pl.when(half != 0)(second.start)
        c_waits.append(first)
    for here in copies[1:]:
        for copy in here:
            copy.start()
    acc[...] = acc_in[...]
    for i in range(n_chunks):
        for copy in copies[i]:
            copy.wait()
        for s in range(n_slots):
            if i == 0:
                m_waits[s].wait()
            lhs = m_buf[s].reshape(-1, depth)
            re_side = jnp.dot(lhs, w_buf[i, 0], preferred_element_type=jnp.float32)
            im_side = jnp.dot(lhs, w_buf[i, 1], preferred_element_type=jnp.float32)
            if i == 0:
                c_waits[s].wait()
            k_count, both = m_buf.shape[1], m_buf.shape[2]
            half_count = both // 2
            for k in range(k_count):
                top = slice(k * both, k * both + half_count)
                low = slice(k * both + half_count, (k + 1) * both)
                left = jnp.concatenate([re_side[top] + im_side[low], im_side[top] - re_side[low]], axis=0)
                high_part = left.astype(jnp.bfloat16)
                low_part = (left - high_part.astype(jnp.float32)).astype(jnp.bfloat16)
                matched = c_buf[s, (k + shift) % k_count, :, i * width : (i + 1) * width]
                dims = (((1,), (1,)), ((), ()))
                added = lax.dot_general(high_part, matched, dims, preferred_element_type=jnp.float32)
                added += lax.dot_general(low_part, matched, dims, preferred_element_type=jnp.float32)
                acc[slots[s], k] = acc[slots[s], k] + added


def add_terms(acc, flags, w_chunks, first_chunk, slots, carried, swapped, matched, near):
    n_chunks, n_slots = len(w_chunks), len(slots)
    _, rows, width = w_chunks[0][0].shape
    k_count, both, depth = carried[0].shape
    span = n_chunks * width
    if n_chunks == CHUNKS:
        pieces = matched
    else:
        pieces = [m[:, :, first_chunk * width : first_chunk * width + span] for m in matched]
    operands = [ref for blocks in w_chunks for ref in blocks]
    operands += [carried[s] for s in slots] + [swapped[s] for s in slots]
    operands += [pieces[(s + 1) % 4] for s in slots] + [pieces[(s - 1) % 4] for s in slots]
    flops = n_chunks * n_slots * (2 * 2 * k_count * both * depth * width + 4 * k_count * both * both * width)
    moved_bytes = n_chunks * 4 * depth * width + n_slots * 2 * k_count * both * (depth + span) + 2 * acc.size * 4
    whole = pl.BlockSpec(memory_space=pltpu.VMEM)
    return pl.pallas_call(
        functools.partial(terms_kernel, n_chunks=n_chunks, slots=tuple(slots), near=near),
        out_shape=jax.ShapeDtypeStruct(acc.shape, acc.dtype),
        in_specs=[pl.BlockSpec(memory_space=pltpu.SMEM)] + [pl.BlockSpec(memory_space=pl.ANY)] * len(operands) + [whole],
        out_specs=whole,
        scratch_shapes=[
            pltpu.VMEM((n_chunks, 2, depth, width), jnp.bfloat16),
            pltpu.VMEM((n_slots, k_count, both, depth), jnp.bfloat16),
            pltpu.VMEM((n_slots, k_count, both, span), jnp.bfloat16),
            pltpu.SemaphoreType.DMA((n_chunks, 5)),
            pltpu.SemaphoreType.DMA((n_slots,)),
            pltpu.SemaphoreType.DMA((n_slots,)),
        ],
        compiler_params=pltpu.CompilerParams(vmem_limit_bytes=56 * 1024 * 1024),
        cost_estimate=pl.CostEstimate(flops=flops, bytes_accessed=moved_bytes, transcendentals=0),
        name="terms",
    )(flags, *operands, acc)


def body(densities, screened, partner, pair_order):
    k_count, n_rows, both = densities.shape
    pair_count = both // 2
    quarter = n_rows // 4
    width = quarter // CHUNKS
    k_owner = lax.axis_index("ka")
    c = lax.axis_index("ga")
    z, b = k_owner // 4, k_owner % 4
    half, odd = z // 2, z % 2
    at_end = (z == 0) | (z == 3)
    own_near = c == odd
    offset = partner[0] % k_count
    flags = jnp.stack([b, own_near.astype(jnp.int32), half, offset]).astype(jnp.int32)

    kept_half = lax.dynamic_slice_in_dim(screened, c * quarter, quarter, 2)
    given_half = lax.dynamic_slice_in_dim(screened, (1 - c) * quarter, quarter, 2)

    def cut(value, n):
        return value[:, :, n * width : (n + 1) * width]

    near_chunks, far_chunks = [], []
    for n in range(CHUNKS):
        kept, given = cut(kept_half, n), cut(given_half, n)
        near_chunks.append(in_plane(jnp.where(own_near, kept, other_core(given))))
    for n in range(CHUNKS):
        kept, given = cut(kept_half, n), cut(given_half, n)
        straight = moved(kept, lambda z, b, c: (z ^ 1, b, c) if c != z % 2 else None)
        crossed = moved(given, lambda z, b, c: (z ^ 1, b, 1 - c) if c != z % 2 else None)
        far_chunks.append(in_plane(jnp.where(own_near, straight, crossed)))

    def own_part(number):
        part = lax.dynamic_slice_in_dim(densities, number * quarter, quarter, 1)
        return jnp.swapaxes(part, 1, 2)

    own_first = own_part(2 * (1 - odd) + c)
    own_second = own_part(2 * odd + c)
    pair_a = end_with_mid(own_first)
    mid_a = mid_with_mid(own_second)
    pair_b = end_with_mid(jnp.where(at_end, own_second, mid_a))
    mid_b = mid_with_mid(pair_a)
    mid_c = mid_with_mid(pair_b)
    pair_c = mid_to_end(mid_b)
    mid_d = mid_with_mid(own_first)
    carried = [
        jnp.where(at_end, own_second, own_first),
        jnp.where(at_end, pair_a, mid_a),
        jnp.where(at_end, pair_b, mid_b),
        jnp.where(at_end, pair_c, pair_b),
    ]
    matched = [
        own_second,
        jnp.where(at_end, pair_a, mid_d),
        jnp.where(at_end, pair_b, mid_c),
        jnp.where(at_end, pair_c, pair_a),
    ]
    swapped = [other_core(part) for part in carried]

    acc = jnp.zeros((4, k_count, both, both), jnp.float32)

    def add(acc, chunks, first, count, slots, near):
        return add_terms(acc, flags, chunks[first : first + count], first, slots, carried, swapped, matched, near)

    for n in range(CHUNKS):
        acc = add(acc, near_chunks, n, 1, (0, 1), True)
    acc = add(acc, near_chunks, 0, CHUNKS, (2,), True)
    for n in range(CHUNKS):
        acc = add(acc, far_chunks, n, 1, (0, 1, 2), False)
    acc = add(acc, near_chunks, 0, CHUNKS, (3,), True)
    acc = add(acc, far_chunks, 0, CHUNKS, (3,), False)

    block_re = acc[:, :, :pair_count, :pair_count] - acc[:, :, pair_count:, pair_count:]
    block_im = acc[:, :, :pair_count, pair_count:] + acc[:, :, pair_count:, :pair_count]
    blocks = jnp.concatenate([block_re, block_im], axis=3)
    blocks = blocks + other_core(blocks)
    total = blocks[0]
    for shift in (1, 2, 3):
        sent = jnp.where(half == 0, blocks[shift], blocks[4 - shift])
        total = total + moved(sent, lambda z, b, c: ((z + shift) % 4, b, c))
    order_table = (jnp.arange(pair_count)[:, None] == pair_order[None, :]).astype(jnp.float32)
    direct = reorder(total[:, :, :pair_count], total[:, :, pair_count:], order_table)
    received = moved(direct, lambda z, b, c: ((z + 1) % 4, b, c))
    sources = (jnp.arange(k_count) - offset) % k_count
    mirror = conjugate_side(jnp.take(received, sources, axis=0), pair_count)
    return (direct, mirror)


def solution(mesh):
    in_specs = (P("ka", None, None), P(None, "ka", "ga"), P(), P())
    out_specs = (P("ka", None, None), P("ka", None, None))
    planes = mesh.shape["ka"] == 16 and mesh.shape["ga"] == 2
    chosen = body if planes else general_body
    return jax.shard_map(chosen, mesh=mesh, in_specs=in_specs, out_specs=out_specs, check_vma=False)
```

```python
import functools

import jax
import jax.numpy as jnp
from jax import lax
from jax.experimental import pallas as pl
from jax.experimental.pallas import tpu as pltpu
from jax.sharding import PartitionSpec as P


def passed_along(value, axis, steps):
    count = lax.axis_size(axis)
    pairs = [(source, (source + steps) % count) for source in range(count)]
    return lax.ppermute(value, axis, pairs)


def conjugate_side(blocks, pair_count):
    real_half = jnp.swapaxes(blocks[:, :, :pair_count], 1, 2)
    imag_half = jnp.swapaxes(blocks[:, :, pair_count:], 1, 2)
    return jnp.concatenate([real_half, -imag_half], axis=2)


def combine_terms(partial_value, order_table, pair_count):
    block_re = partial_value[:, 0, :, :pair_count] - partial_value[:, 1, :, pair_count:]
    block_im = partial_value[:, 0, :, pair_count:] + partial_value[:, 1, :, :pair_count]
    return reorder(block_re, block_im, order_table)


def reorder(block_re, block_im, order_table):
    block_re = jnp.einsum("kpq,qj->kpj", block_re, order_table, precision=lax.Precision.HIGHEST)
    block_im = jnp.einsum("kpq,qj->kpj", block_im, order_table, precision=lax.Precision.HIGHEST)
    return jnp.concatenate([block_re, block_im], axis=2)


def finish_terms(left_sums, matched, pair_count):
    left_re = left_sums[:, 0, :pair_count] + left_sums[:, 1, pair_count:]
    left_im = left_sums[:, 1, :pair_count] - left_sums[:, 0, pair_count:]
    left_factor = jnp.stack([left_re, left_im], axis=1)
    return jnp.einsum(
        "kwpc,kcq->kwpq", left_factor, matched.astype(jnp.float32), precision=lax.Precision.HIGHEST
    )


def general_body(densities, screened, partner, pair_order):
    k_count = densities.shape[0]
    pair_count = densities.shape[2] // 2
    panel_width = screened.shape[2]
    k_owner = lax.axis_index("ka")
    column = lax.axis_index("ga")
    own_columns = lax.dynamic_slice_in_dim(densities, column * panel_width, panel_width, 1)
    arrived = passed_along(own_columns, "ka", -4)
    own_partner = lax.dynamic_slice_in_dim(partner, k_owner * k_count, k_count, 0)
    slot_index = own_partner % k_count
    offset = slot_index[0]
    matched = jnp.take(arrived, slot_index, axis=0)
    left_sums = jnp.einsum(
        "kgp,wgc->kwpc",
        densities,
        lax.all_gather(screened, "ka", axis=1, tiled=True),
        preferred_element_type=jnp.float32,
    )
    partial_value = finish_terms(left_sums, matched, pair_count)
    order_table = (jnp.arange(pair_count)[:, None] == pair_order[None, :]).astype(jnp.float32)
    sources = (jnp.arange(k_count) - offset) % k_count
    summed = lax.psum(partial_value, "ga")
    direct = combine_terms(summed, order_table, pair_count)
    received = passed_along(direct, "ka", 4)
    mirror = conjugate_side(jnp.take(received, sources, axis=0), pair_count)
    return (direct, mirror)


AXES = ("ka", "ga")
STEP = 256
WIDE_STEP = 512


def device(z, b, c):
    return (z * 4 + b) * 2 + c


def moved(value, rule):
    pairs = []
    for z in range(4):
        for b in range(4):
            for c in range(2):
                target = rule(z, b, c)
                if target is not None:
                    pairs.append((device(z, b, c), device(*target)))
    return lax.ppermute(value, AXES, pairs)


def along_x(value):
    return moved(value, lambda z, b, c: (z, b ^ 1, c))


def along_y(value):
    return moved(value, lambda z, b, c: (z, b ^ 2, c))


def other_core(value):
    return moved(value, lambda z, b, c: (z, b, 1 - c))


def end_with_mid(value):
    return moved(value, lambda z, b, c: (z ^ 1, b, c))


def mid_to_end(value):
    return moved(value, lambda z, b, c: (z ^ 1, b, c) if z in (1, 2) else None)


def mid_with_mid(value):
    return moved(value, lambda z, b, c: (3 - z, b, c) if z in (1, 2) else None)


ANYWHERE = pl.BlockSpec(memory_space=pltpu.HBM)
IN_SMEM = pl.BlockSpec(memory_space=pltpu.SMEM)
IN_VMEM = pl.BlockSpec(memory_space=pltpu.VMEM)
PARAMS = pltpu.CompilerParams(vmem_limit_bytes=60 * 1024 * 1024)
COST = pl.CostEstimate(flops=1000, bytes_accessed=1000, transcendentals=0)
FLAGS = jax.ShapeDtypeStruct((8,), jnp.int32)


def keep_flags(flags, out):
    for i in range(flags.shape[0]):
        out[i] = flags[i]


def always(flags):
    return None


def at_end(flags):
    return flags[4] == 1


def at_mid(flags):
    return flags[4] == 0


def own_near(flags):
    return flags[1] == 1


def own_far(flags):
    return flags[1] == 0


def whole(ref):
    return ref


def real(first, width):
    return lambda ref: ref.at[0, :, first : first + width]


def imaginary(first, width):
    return lambda ref: ref.at[1, :, first : first + width]


def columns_of(first, width):
    return lambda ref: ref.at[:, first : first + width]


def moves_kernel(flags, *refs, plan, n_sources, n_outs, n_passing):
    sources, outs = refs[:n_sources], refs[n_sources : n_sources + n_outs]
    flags_out, *stages = refs[n_sources + n_outs + n_passing : -2]
    in_sems, out_sems = refs[-2:]

    def run(chosen, act):
        if chosen is None:
            act()
        else:
            pl.when(chosen)(act)

    copies = []
    for i, (when, number, view, out_number, target) in enumerate(plan):
        stage = target(stages[out_number])
        load = pltpu.make_async_copy(view(sources[number]), stage, in_sems.at[i])
        store = pltpu.make_async_copy(stage, target(outs[out_number]), out_sems.at[i])
        copies.append((when(flags), load, store))
        run(when(flags), load.start)
    keep_flags(flags, flags_out)
    for chosen, load, store in copies:
        def forward():
            load.wait()
            store.start()

        run(chosen, forward)
    for chosen, _, store in copies:
        run(chosen, store.wait)


def moves(flags, waits, *outputs, passing=()):
    sources, plan = [], []
    for number, (_, pieces) in enumerate(outputs):
        for when, source, view, target in pieces:
            plan.append((when, len(sources), view, number, target))
            sources.append(source)
    operands = sources + list(waits)
    shapes = [jax.ShapeDtypeStruct(shape, jnp.bfloat16) for shape, _ in outputs]
    aliases = {1 + len(operands) + i: len(outputs) + i for i in range(len(passing))}
    operands += list(passing)
    shapes += [jax.ShapeDtypeStruct(value.shape, value.dtype) for value in passing]
    results = pl.pallas_call(
        functools.partial(
            moves_kernel, plan=tuple(plan), n_sources=len(operands), n_outs=len(outputs), n_passing=len(passing)
        ),
        out_shape=tuple(shapes) + (FLAGS,),
        in_specs=[IN_SMEM] + [ANYWHERE] * len(operands),
        out_specs=(ANYWHERE,) * len(shapes) + (IN_SMEM,),
        input_output_aliases=aliases,
        scratch_shapes=[pltpu.VMEM(shape, jnp.bfloat16) for shape, _ in outputs]
        + [pltpu.SemaphoreType.DMA((max(len(plan), 1),))] * 2,
        compiler_params=PARAMS,
        cost_estimate=COST,
        name="moves",
    )(flags, *operands)
    return results[-1], *results[:-1]


def w_copies(blocks, places, own_b, w_buf, source_at, target_at, step, sems):
    width, real_at, imaginary_at = places
    own, x_side, y_side, d_re, d_im = blocks
    rows = own.shape[0]
    copies = []

    def add(source, first, part, turn):
        start = pl.multiple_of((own_b ^ turn) * rows, rows)
        target = w_buf.at[part, pl.ds(start, rows), target_at : target_at + step]
        source = source.at[:, first + source_at : first + source_at + step]
        copies.append(pltpu.make_async_copy(source, target, sems.at[len(copies)]))

    for turn, source in ((0, own), (1, x_side), (2, y_side)):
        add(source, 0, 0, turn)
        add(source, width, 1, turn)
    add(d_re, real_at, 0, 3)
    add(d_im, imaginary_at, 1, 3)
    return copies


def either(chosen, first, second, target, sem):
    a = pltpu.make_async_copy(first, target, sem)
    b = pltpu.make_async_copy(second, target, sem)
    pl.when(chosen)(a.start)
    pl.when(jnp.logical_not(chosen))(b.start)
    return a


def matched_copies(flags, matched, c_buf, first, width, sems):
    n_slots = c_buf.shape[0]
    slot_0, slot_2, near_one, far_one = [matched[2 * i : 2 * i + 2] for i in range(4)]
    quarter = slot_0[0].shape[2]
    for s in range(n_slots):
        for half, s_matched in ((0, (s + 1) % n_slots), (1, (s - 1) % n_slots)):
            for end, ordered in ((1, (slot_0, near_one, slot_2, far_one)), (0, (slot_0, far_one, slot_2, near_one))):
                for number in range(2):
                    low, high = max(first, number * quarter), min(first + width, (number + 1) * quarter)
                    if low >= high:
                        continue
                    for core in range(2):
                        source = ordered[s_matched][0 if core == number else 1]
                        copy = pltpu.make_async_copy(
                            source.at[:, :, low - number * quarter : high - number * quarter],
                            c_buf.at[s, :, :, low - first : high - first],
                            sems.at[s],
                        )
                        pl.when((flags[2] == half) & (flags[4] == end) & (flags[5] == core))(copy.start)


def matched_wait(c_buf, s, sems):
    pltpu.make_async_copy(c_buf.at[s], c_buf.at[s], sems.at[s]).wait()


def left_tile(lhs, w_re, w_im, k_count, both):
    re_side = jnp.dot(lhs, w_re, preferred_element_type=jnp.float32).reshape(k_count, both, -1)
    im_side = jnp.dot(lhs, w_im, preferred_element_type=jnp.float32).reshape(k_count, both, -1)
    pairs = both // 2
    left_re = re_side[:, :pairs] + im_side[:, pairs:]
    left_im = im_side[:, :pairs] - re_side[:, pairs:]
    return jnp.concatenate([left_re, left_im], axis=1)


def times_matched(left, matched):
    high_part = left.astype(jnp.bfloat16)
    low_part = (left - high_part.astype(jnp.float32)).astype(jnp.bfloat16)
    rows = left.shape[0]
    both_parts = jnp.concatenate([high_part, low_part], axis=0)
    dims = (((1,), (1,)), ((), ()))
    added = lax.dot_general(both_parts, matched, dims, preferred_element_type=jnp.float32)
    return added[:rows] + added[rows:]


def first_kernel(flags, *refs, first_slot, n_slots, columns, places, step, fresh):
    n_chunks = len(columns)
    w_refs = [refs[5 * i : 5 * i + 5] for i in range(n_chunks)]
    rest = refs[5 * n_chunks :]
    of_end, of_mid = rest[:n_slots], rest[n_slots : 2 * n_slots]
    rest = rest[2 * n_slots :]
    if not fresh:
        rest = rest[1:]
    left, flags_out, w_buf, m_buf, out_buf, w_sems, m_sems, out_sems = rest
    depth = w_buf.shape[1]
    _, k_count, both, _ = m_buf.shape
    base = columns[0][0]
    copies, used = [], 0
    for i in range(n_chunks):
        for at in range(0, columns[i][1], step):
            copies.append(w_copies(w_refs[i], places[i], flags[0], w_buf, at, used, step, w_sems.at[used // step]))
            used += step
    total = n_slots * (used // step)
    for copy in copies[0]:
        copy.start()
    for s in range(n_slots):
        either(at_end(flags), of_end[s], of_mid[s], m_buf.at[s], m_sems.at[s])
    for here in copies[1:]:
        for copy in here:
            copy.start()
    keep_flags(flags, flags_out)

    def out_copy(t):
        start = pl.multiple_of(base + (t // n_slots) * step, STEP)
        target = left.at[first_slot + t % n_slots, :, :, pl.ds(start, step)]
        return pltpu.make_async_copy(out_buf.at[t % 2], target, out_sems.at[t % 2])

    def one_step(t, carry):
        @pl.when(t >= 2)
        def _():
            out_copy(t - 2).wait()

        tile_number, s = t // n_slots, t % n_slots
        start = pl.multiple_of(tile_number * step, step)

        @pl.when(s == 0)
        def _():
            for copy in w_copies(w_refs[0], places[0], flags[0], w_buf, 0, 0, step, w_sems.at[tile_number]):
                copy.wait()

        @pl.when(tile_number == 0)
        def _():
            pltpu.make_async_copy(of_end[0], m_buf.at[s], m_sems.at[s]).wait()

        lhs = m_buf[s].reshape(k_count * both, depth)
        out_buf[t % 2] = left_tile(lhs, w_buf[0, :, pl.ds(start, step)], w_buf[1, :, pl.ds(start, step)], k_count, both)
        out_copy(t).start()
        return carry

    lax.fori_loop(0, total, one_step, 0)
    for t in range(max(total - 2, 0), total):
        out_copy(t).wait()


def first_product(flags, chunks, first_slot, n_slots, of_end, of_mid, left, all_columns):
    depth = 4 * chunks[0][2][0].shape[0]
    k_count, both, _ = of_end[first_slot].shape
    columns = tuple((first, width) for first, width, _, _ in chunks)
    span = sum(width for _, width in columns)
    slots = range(first_slot, first_slot + n_slots)
    step = WIDE_STEP if all(width % WIDE_STEP == 0 for _, width in columns) else STEP
    operands = [ref for _, _, blocks, _ in chunks for ref in blocks]
    operands += [of_end[s] for s in slots] + [of_mid[s] for s in slots]
    aliases = {}
    if left is not None:
        operands.append(left)
        aliases = {len(operands): 0}
    whole = jax.ShapeDtypeStruct((4, k_count, both, all_columns), jnp.float32)
    return pl.pallas_call(
        functools.partial(
            first_kernel, first_slot=first_slot, n_slots=n_slots, columns=columns, step=step, fresh=left is None,
            places=tuple(places for _, _, _, places in chunks),
        ),
        out_shape=(whole, FLAGS),
        in_specs=[IN_SMEM] + [ANYWHERE] * len(operands),
        out_specs=(ANYWHERE, IN_SMEM),
        input_output_aliases=aliases,
        scratch_shapes=[
            pltpu.VMEM((2, depth, span), jnp.bfloat16),
            pltpu.VMEM((n_slots, k_count, both, depth), jnp.bfloat16),
            pltpu.VMEM((2, k_count, both, step), jnp.float32),
            pltpu.SemaphoreType.DMA((span // step, 8)),
            pltpu.SemaphoreType.DMA((n_slots,)),
            pltpu.SemaphoreType.DMA((2,)),
        ],
        compiler_params=PARAMS,
        cost_estimate=COST,
        name="first_product",
    )(flags, *operands)


def second_kernel(flags, left, *refs, base, width):
    matched = refs[:8]
    sums, flags_out, left_buf, c_buf, left_sems, c_sems = refs[8:]
    shift = flags[3]
    n_slots, k_count = c_buf.shape[:2]
    window = slice(base, base + width)

    def left_copy(t):
        source = left.at[t // k_count, t % k_count, :, window]
        return pltpu.make_async_copy(source, left_buf.at[t % 4], left_sems.at[t % 4])

    for t in range(4):
        left_copy(t).start()
    matched_copies(flags, matched, c_buf, base, width, c_sems)
    keep_flags(flags, flags_out)

    def step(t, carry):
        s, k = t // k_count, t % k_count

        @pl.when(k == 0)
        def _():
            matched_wait(c_buf, s, c_sems)

        left_copy(t).wait()
        sums[s, k] = times_matched(left_buf[t % 4], c_buf[s, (k + shift) % k_count])

        @pl.when(t + 4 < n_slots * k_count)
        def _():
            left_copy(t + 4).start()

        return carry

    lax.fori_loop(0, n_slots * k_count, step, 0)


def second_product(flags, left, matched, base, width):
    n_slots, k_count, both, _ = left.shape
    return pl.pallas_call(
        functools.partial(second_kernel, base=base, width=width),
        out_shape=(jax.ShapeDtypeStruct((n_slots, k_count, both, both), jnp.float32), FLAGS),
        in_specs=[IN_SMEM] + [ANYWHERE] * (1 + len(matched)),
        out_specs=(IN_VMEM, IN_SMEM),
        scratch_shapes=[
            pltpu.VMEM((4, both, width), jnp.float32),
            pltpu.VMEM((n_slots, k_count, both, width), jnp.bfloat16),
            pltpu.SemaphoreType.DMA((4,)),
            pltpu.SemaphoreType.DMA((n_slots,)),
        ],
        compiler_params=PARAMS,
        cost_estimate=COST,
        name="second_product",
    )(flags, left, *matched)


def last_kernel(flags, *refs, n_slots, base, places):
    w_refs, rest = refs[:5], refs[5:]
    of_end, of_mid, rest = rest[:n_slots], rest[n_slots : 2 * n_slots], rest[2 * n_slots :]
    matched, rest = rest[:8], rest[8:]
    sums, blocks, w_buf, m_buf, c_buf, w_sems, m_sems, c_sems = rest
    shift = flags[3]
    depth, width = w_buf.shape[1:]
    _, k_count, both, _ = m_buf.shape
    pairs = both // 2
    copies = w_copies(w_refs, places, flags[0], w_buf, 0, 0, width, w_sems)
    for copy in copies:
        copy.start()
    for s in range(n_slots):
        either(at_end(flags), of_end[s], of_mid[s], m_buf.at[s], m_sems.at[s])
    matched_copies(flags, matched, c_buf, base, width, c_sems)
    for copy in copies:
        copy.wait()

    def step(s, carry):
        pltpu.make_async_copy(of_end[0], m_buf.at[s], m_sems.at[s]).wait()
        matched_wait(c_buf, s, c_sems)
        lhs = m_buf[s].reshape(k_count * both, depth)
        tile = left_tile(lhs, w_buf[0], w_buf[1], k_count, both)
        for k in range(k_count):
            terms = sums[s, k] + times_matched(tile[k], c_buf[s, (k + shift) % k_count])
            blocks[s, k, :, :pairs] = terms[:pairs, :pairs] - terms[pairs:, pairs:]
            blocks[s, k, :, pairs:] = terms[:pairs, pairs:] + terms[pairs:, :pairs]
        return carry

    lax.fori_loop(0, n_slots, step, 0)


def last_product(flags, chunk, of_end, of_mid, matched, sums):
    n_slots, k_count, both, _ = sums.shape
    base, width, w_blocks, places = chunk
    depth = 4 * w_blocks[0].shape[0]
    operands = list(w_blocks) + list(of_end) + list(of_mid) + list(matched)
    return pl.pallas_call(
        functools.partial(last_kernel, n_slots=n_slots, base=base, places=places),
        out_shape=jax.ShapeDtypeStruct((n_slots, k_count, both // 2, both), jnp.float32),
        in_specs=[IN_SMEM] + [ANYWHERE] * len(operands) + [IN_VMEM],
        out_specs=IN_VMEM,
        scratch_shapes=[
            pltpu.VMEM((2, depth, width), jnp.bfloat16),
            pltpu.VMEM((n_slots, k_count, both, depth), jnp.bfloat16),
            pltpu.VMEM((n_slots, k_count, both, width), jnp.bfloat16),
            pltpu.SemaphoreType.DMA((8,)),
            pltpu.SemaphoreType.DMA((n_slots,)),
            pltpu.SemaphoreType.DMA((n_slots,)),
        ],
        compiler_params=PARAMS,
        cost_estimate=COST,
        name="last_product",
    )(flags, *operands, sums)


def turn_kernel(flags, first, second, first_turned, second_turned):
    first_turned[0] = first[0].T
    second_turned[0] = second[0].T


def turned_parts(flags, densities):
    k_count, n_rows, both = densities.shape
    quarter = n_rows // 4
    turned = jax.ShapeDtypeStruct((k_count, both, quarter), densities.dtype)

    def part(which):
        return pl.BlockSpec((1, quarter, both), lambda k, flags: (k, flags[which], 0))

    out = pl.BlockSpec((1, both, quarter), lambda k, flags: (k, 0, 0))
    return pl.pallas_call(
        turn_kernel,
        out_shape=(turned, turned),
        grid_spec=pltpu.PrefetchScalarGridSpec(
            num_scalar_prefetch=1, grid=(k_count,), in_specs=[part(6), part(7)], out_specs=[out, out]
        ),
        compiler_params=PARAMS,
        cost_estimate=COST,
        name="turned_parts",
    )(flags, densities, densities)


def body(densities, screened, partner, pair_order):
    k_count, n_rows, both = densities.shape
    pair_count = both // 2
    quarter = n_rows // 4
    panel = screened.shape[2]
    widths = (panel // 4, 5 * panel // 12, panel // 4, panel // 12)
    firsts = [sum(widths[:n]) for n in range(4)]
    k_owner = lax.axis_index("ka")
    c = lax.axis_index("ga")
    z, b = k_owner // 4, k_owner % 4
    half, odd = z // 2, z % 2
    offset = partner[0] % k_count
    ends = (z == 0) | (z == 3)
    flags = jnp.stack([b, c == odd, half, offset, ends, c, 2 * (1 - odd) + c, 2 * odd + c]).astype(jnp.int32)
    rows = screened.shape[1]

    part = (k_count, both, quarter)

    def own_pieces(n, when, at=0):
        first, width = firsts[n], widths[n]
        return [
            (when, screened, real(first, width), columns_of(at, width)),
            (when, screened, imaginary(first, width), columns_of(at + width, width)),
        ]

    def far_part(*numbers):
        pieces, at = [], 0
        for n in numbers:
            pieces += own_pieces(n, own_far, at)
            at += 2 * widths[n]
        return (rows, at), pieces

    def sent_far(value):
        return moved(value, lambda z, b, c: (z ^ 1, b, 1 - c) if c != z % 2 else None)

    def panel_parts(n, arrived, at=0, before=None):
        pieces = own_pieces(n, own_near) + [(own_far, arrived, columns_of(at, 2 * widths[n]), columns_of(0, 2 * widths[n]))]
        if before is None:
            return (((rows, 2 * widths[n]), pieces),)
        x_side, y_side = before
        passed = widths[n - 1]
        shape, place = (rows, 2 * widths[n] + passed), columns_of(2 * widths[n], passed)
        return (
            (shape, pieces + [(always, y_side, columns_of(passed, passed), place)]),
            (shape, pieces + [(always, x_side, columns_of(0, passed), place)]),
        )

    def end_or_mid(end, mid):
        return part, [(at_end, end, whole, whole), (at_mid, mid, whole, whole)]

    flags, sent_0, sent_1 = moves(flags, (), far_part(0), far_part(1))
    arrived_0, arrived_1 = sent_far(sent_0), sent_far(sent_1)
    own_first, own_second = turned_parts(flags, densities)
    pair_a, mid_a = end_with_mid(own_first), mid_with_mid(own_second)
    swapped_0 = other_core(own_second)

    flags, panel_0 = moves(flags, (swapped_0,), *panel_parts(0, arrived_0))
    x_0, y_0 = along_x(panel_0), along_y(panel_0)

    flags, to_x, to_y, sent_2, to_mid = moves(
        flags,
        (mid_a,),
        *panel_parts(1, arrived_1, 0, (x_0, y_0)),
        far_part(2, 3),
        (part, [(always, own_first, whole, whole)]),
    )
    x_1, y_1 = along_x(to_x), along_y(to_y)
    panel_1 = to_x
    arrived_2 = sent_far(sent_2)
    mid_d = mid_with_mid(to_mid)

    flags, to_pair, pair_a = moves(flags, (), end_or_mid(own_second, mid_a), passing=(pair_a,))
    pair_b = end_with_mid(to_pair)

    flags, to_mid = moves(flags, (mid_d,), (part, [(always, pair_a, whole, whole)]))
    mid_b = mid_with_mid(to_mid)

    flags, to_x, to_y, pair_a = moves(flags, (), *panel_parts(2, arrived_2, 0, (x_1, y_1)), passing=(pair_a,))
    x_2, y_2 = along_x(to_x), along_y(to_y)
    panel_2 = to_x
    swapped_a = other_core(pair_a)
    chunk_0 = (firsts[0], widths[0], (panel_0, x_0, y_0, y_1, x_1), (widths[0], 2 * widths[1], 2 * widths[1]))
    of_end, of_mid = [own_second, pair_a, None, None], [own_first, mid_a, None, None]
    left, flags = first_product(flags, [chunk_0], 0, 2, of_end, of_mid, None, panel)

    flags, pair_b, mid_b = moves(flags, (), passing=(pair_b, mid_b))
    of_end[2], of_mid[2], of_mid[3] = pair_b, mid_b, pair_b
    pair_c, mid_c = mid_to_end(mid_b), mid_with_mid(pair_b)
    left, flags = first_product(flags, [chunk_0], 2, 1, of_end, of_mid, left, panel)

    flags, to_x, to_y = moves(flags, (swapped_a,), *panel_parts(3, arrived_2, 2 * widths[2], (x_2, y_2)))
    x_3, y_3 = along_x(to_x), along_y(to_y)
    panel_3 = to_x
    chunk_1 = (firsts[1], widths[1], (panel_1, x_1, y_1, y_2, x_2), (widths[1], 2 * widths[2], 2 * widths[2]))
    left, flags = first_product(flags, [chunk_1], 0, 3, of_end, of_mid, left, panel)

    flags, carried_2, carried_3 = moves(flags, (), end_or_mid(pair_b, mid_c), end_or_mid(pair_c, mid_d))
    swapped_2, swapped_3 = other_core(carried_2), other_core(carried_3)
    of_end[3] = pair_c
    left, flags = first_product(flags, [chunk_0, chunk_1], 3, 1, of_end, of_mid, left, panel)

    shape = (rows, widths[3])
    flags, to_x, to_y = moves(
        flags,
        (),
        (shape, [(always, y_3, columns_of(widths[3], widths[3]), whole)]),
        (shape, [(always, x_3, columns_of(0, widths[3]), whole)]),
    )
    x_4, y_4 = along_x(to_x), along_y(to_y)
    chunk_2 = (firsts[2], widths[2], (panel_2, x_2, y_2, y_3, x_3), (widths[2], 2 * widths[3], 2 * widths[3]))
    left, flags = first_product(flags, [chunk_2], 0, 4, of_end, of_mid, left, panel)
    matched = [own_second, swapped_0, carried_2, swapped_2, pair_a, swapped_a, carried_3, swapped_3]
    sums, flags = second_product(flags, left, matched, 0, firsts[3])
    last = (firsts[3], widths[3], (panel_3, x_3, y_3, y_4, x_4), (widths[3], 0, 0))
    blocks = last_product(flags, last, of_end, of_mid, matched, sums)

    blocks = blocks + other_core(blocks)
    total = blocks[0]
    for shift in (1, 2, 3):
        sent = jnp.where(half == 0, blocks[shift], blocks[4 - shift])
        total = total + moved(sent, lambda z, b, c: ((z + shift) % 4, b, c))
    order_table = (jnp.arange(pair_count)[:, None] == pair_order[None, :]).astype(jnp.float32)
    direct = reorder(total[:, :, :pair_count], total[:, :, pair_count:], order_table)
    received = moved(direct, lambda z, b, c: ((z + 1) % 4, b, c))
    sources = (jnp.arange(k_count) - offset) % k_count
    mirror = conjugate_side(jnp.take(received, sources, axis=0), pair_count)
    return (direct, mirror)


def solution(mesh):
    in_specs = (P("ka", None, None), P(None, "ka", "ga"), P(), P())
    out_specs = (P("ka", None, None), P("ka", None, None))
    planes = mesh.shape["ka"] == 16 and mesh.shape["ga"] == 2
    chosen = body if planes else general_body
    return jax.shard_map(chosen, mesh=mesh, in_specs=in_specs, out_specs=out_specs, check_vma=False)
```

```python
import functools

import jax
import jax.numpy as jnp
from jax import lax
from jax.experimental import pallas as pl
from jax.experimental.pallas import tpu as pltpu
from jax.sharding import PartitionSpec as P


def passed_along(value, axis, steps):
    count = lax.axis_size(axis)
    pairs = [(source, (source + steps) % count) for source in range(count)]
    return lax.ppermute(value, axis, pairs)


def conjugate_side(blocks, pair_count):
    real_half = jnp.swapaxes(blocks[:, :, :pair_count], 1, 2)
    imag_half = jnp.swapaxes(blocks[:, :, pair_count:], 1, 2)
    return jnp.concatenate([real_half, -imag_half], axis=2)


def combine_terms(partial_value, order_table, pair_count):
    block_re = partial_value[:, 0, :, :pair_count] - partial_value[:, 1, :, pair_count:]
    block_im = partial_value[:, 0, :, pair_count:] + partial_value[:, 1, :, :pair_count]
    return reorder(block_re, block_im, order_table)


def reorder(block_re, block_im, order_table):
    block_re = jnp.einsum("kpq,qj->kpj", block_re, order_table, precision=lax.Precision.HIGHEST)
    block_im = jnp.einsum("kpq,qj->kpj", block_im, order_table, precision=lax.Precision.HIGHEST)
    return jnp.concatenate([block_re, block_im], axis=2)


def finish_terms(left_sums, matched, pair_count):
    left_re = left_sums[:, 0, :pair_count] + left_sums[:, 1, pair_count:]
    left_im = left_sums[:, 1, :pair_count] - left_sums[:, 0, pair_count:]
    left_factor = jnp.stack([left_re, left_im], axis=1)
    return jnp.einsum(
        "kwpc,kcq->kwpq", left_factor, matched.astype(jnp.float32), precision=lax.Precision.HIGHEST
    )


def general_body(densities, screened, partner, pair_order):
    k_count = densities.shape[0]
    pair_count = densities.shape[2] // 2
    panel_width = screened.shape[2]
    k_owner = lax.axis_index("ka")
    column = lax.axis_index("ga")
    own_columns = lax.dynamic_slice_in_dim(densities, column * panel_width, panel_width, 1)
    arrived = passed_along(own_columns, "ka", -4)
    own_partner = lax.dynamic_slice_in_dim(partner, k_owner * k_count, k_count, 0)
    slot_index = own_partner % k_count
    offset = slot_index[0]
    matched = jnp.take(arrived, slot_index, axis=0)
    left_sums = jnp.einsum(
        "kgp,wgc->kwpc",
        densities,
        lax.all_gather(screened, "ka", axis=1, tiled=True),
        preferred_element_type=jnp.float32,
    )
    partial_value = finish_terms(left_sums, matched, pair_count)
    order_table = (jnp.arange(pair_count)[:, None] == pair_order[None, :]).astype(jnp.float32)
    sources = (jnp.arange(k_count) - offset) % k_count
    summed = lax.psum(partial_value, "ga")
    direct = combine_terms(summed, order_table, pair_count)
    received = passed_along(direct, "ka", 4)
    mirror = conjugate_side(jnp.take(received, sources, axis=0), pair_count)
    return (direct, mirror)


AXES = ("ka", "ga")
STEP = 256
WIDE_STEP = 512


def device(z, b, c):
    return (z * 4 + b) * 2 + c


def moved(value, rule):
    pairs = []
    for z in range(4):
        for b in range(4):
            for c in range(2):
                target = rule(z, b, c)
                if target is not None:
                    pairs.append((device(z, b, c), device(*target)))
    return lax.ppermute(value, AXES, pairs)


def along_x(value):
    return moved(value, lambda z, b, c: (z, b ^ 1, c))


def along_y(value):
    return moved(value, lambda z, b, c: (z, b ^ 2, c))


def other_core(value):
    return moved(value, lambda z, b, c: (z, b, 1 - c))


def end_with_mid(value):
    return moved(value, lambda z, b, c: (z ^ 1, b, c))


def mid_to_end(value):
    return moved(value, lambda z, b, c: (z ^ 1, b, c) if z in (1, 2) else None)


def mid_with_mid(value):
    return moved(value, lambda z, b, c: (3 - z, b, c) if z in (1, 2) else None)


ANYWHERE = pl.BlockSpec(memory_space=pltpu.HBM)
IN_SMEM = pl.BlockSpec(memory_space=pltpu.SMEM)
IN_VMEM = pl.BlockSpec(memory_space=pltpu.VMEM)
PARAMS = pltpu.CompilerParams(vmem_limit_bytes=60 * 1024 * 1024)
COST = pl.CostEstimate(flops=1000, bytes_accessed=1000, transcendentals=0)
FLAGS = jax.ShapeDtypeStruct((8,), jnp.int32)


def keep_flags(flags, out):
    for i in range(flags.shape[0]):
        out[i] = flags[i]


def always(flags):
    return None


def at_end(flags):
    return flags[4] == 1


def at_mid(flags):
    return flags[4] == 0


def own_near(flags):
    return flags[1] == 1


def own_far(flags):
    return flags[1] == 0


def whole(ref):
    return ref


def real(first, width):
    return lambda ref: ref.at[0, :, first : first + width]


def imaginary(first, width):
    return lambda ref: ref.at[1, :, first : first + width]


def columns_of(first, width):
    return lambda ref: ref.at[:, first : first + width]


def slots_from(first, count):
    return lambda ref: ref.at[first : first + count]


def moves_kernel(flags, *refs, plan, n_sources, n_outs, n_passing):
    sources, outs = refs[:n_sources], refs[n_sources : n_sources + n_outs]
    flags_out, *stages = refs[n_sources + n_outs + n_passing : -2]
    in_sems, out_sems = refs[-2:]

    def run(chosen, act):
        if chosen is None:
            act()
        else:
            pl.when(chosen)(act)

    copies = []
    for i, (when, number, view, out_numbers, target) in enumerate(plan):
        stage = target(stages[out_numbers[0]])
        load = pltpu.make_async_copy(view(sources[number]), stage, in_sems.at[i])
        stores = [
            pltpu.make_async_copy(stage, target(outs[out_number]), out_sems.at[i, j])
            for j, out_number in enumerate(out_numbers)
        ]
        copies.append((when(flags), load, stores))
        run(when(flags), load.start)
    keep_flags(flags, flags_out)
    for chosen, load, stores in copies:
        def forward():
            load.wait()
            for store in stores:
                store.start()

        run(chosen, forward)
    for chosen, _, stores in copies:
        for store in stores:
            run(chosen, store.wait)


def moves(flags, waits, *outputs, passing=()):
    sources, plan = [], []
    for number, (_, pieces) in enumerate(outputs):
        for when, source, view, target, *more in pieces:
            plan.append((when, len(sources), view, tuple(range(number, number + 1 + sum(more))), target))
            sources.append(source)
    operands = sources + list(waits)
    shapes = [jax.ShapeDtypeStruct(shape, jnp.bfloat16) for shape, _ in outputs]
    aliases = {1 + len(operands) + i: len(outputs) + i for i in range(len(passing))}
    operands += list(passing)
    shapes += [jax.ShapeDtypeStruct(value.shape, value.dtype) for value in passing]
    results = pl.pallas_call(
        functools.partial(
            moves_kernel, plan=tuple(plan), n_sources=len(operands), n_outs=len(outputs), n_passing=len(passing)
        ),
        out_shape=tuple(shapes) + (FLAGS,),
        in_specs=[IN_SMEM] + [ANYWHERE] * len(operands),
        out_specs=(ANYWHERE,) * len(shapes) + (IN_SMEM,),
        input_output_aliases=aliases,
        scratch_shapes=[pltpu.VMEM(shape, jnp.bfloat16) for shape, _ in outputs]
        + [pltpu.SemaphoreType.DMA((max(len(plan), 1),)), pltpu.SemaphoreType.DMA((max(len(plan), 1), 2))],
        compiler_params=PARAMS,
        cost_estimate=COST,
        name="moves",
    )(flags, *operands)
    return results[-1], *results[:-1]


def w_copies(blocks, places, turns, w_buf, source_at, target_at, step, sems):
    width, real_at, imaginary_at = places
    rows = w_buf.shape[1] // len(turns)
    copies = []
    for i, turn in enumerate(turns):
        for part in range(2):
            source = blocks[turn] if turn < 3 else blocks[3 + part]
            first = (real_at, imaginary_at)[part] if turn == 3 else part * width
            target = w_buf.at[part, i * rows : (i + 1) * rows, target_at : target_at + step]
            source = source.at[:, first + source_at : first + source_at + step]
            copies.append(pltpu.make_async_copy(source, target, sems.at[len(copies)]))
    return copies


def m_copies(flags, turns, end_part, mid_part, target, sem):
    rows = target.shape[2] // len(turns)
    for i, turn in enumerate(turns):
        start = pl.multiple_of((flags[0] ^ turn) * rows, rows)
        window = pl.ds(start, rows)
        place = target.at[:, :, i * rows : (i + 1) * rows]
        either(at_end(flags), end_part.at[:, :, window], mid_part.at[:, :, window], place, sem)


def part_of(ref, lead, count):
    return ref.at[lead : lead + count]


def either(chosen, first, second, target, sem):
    a = pltpu.make_async_copy(first, target, sem)
    b = pltpu.make_async_copy(second, target, sem)
    pl.when(chosen)(a.start)
    pl.when(jnp.logical_not(chosen))(b.start)
    return a


def matched_copies(flags, matched, leads, c_buf, first_slot, first, width, sems):
    n_slots, k_count = c_buf.shape[:2]
    pairs = [[part_of(matched[2 * i + j], leads[2 * i + j], k_count) for j in range(2)] for i in range(4)]
    quarter = matched[0].shape[2]
    for s in range(n_slots):
        for half, s_matched in ((0, (first_slot + s + 1) % 4), (1, (first_slot + s - 1) % 4)):
            for end, order in ((1, (0, 1, 2, 3)), (0, (0, 2, 3, 1))):
                for number in range(2):
                    low, high = max(first, number * quarter), min(first + width, (number + 1) * quarter)
                    if low >= high:
                        continue
                    for core in range(2):
                        source = pairs[order[s_matched]][0 if core == number else 1]
                        copy = pltpu.make_async_copy(
                            source.at[:, :, low - number * quarter : high - number * quarter],
                            c_buf.at[s, :, :, low - first : high - first],
                            sems.at[s],
                        )
                        pl.when((flags[2] == half) & (flags[4] == end) & (flags[5] == core))(copy.start)


def matched_wait(c_buf, s, sems):
    pltpu.make_async_copy(c_buf.at[s], c_buf.at[s], sems.at[s]).wait()


def left_tile(lhs, w_re, w_im, k_count, both):
    re_side = jnp.dot(lhs, w_re, preferred_element_type=jnp.float32).reshape(k_count, both, -1)
    im_side = jnp.dot(lhs, w_im, preferred_element_type=jnp.float32).reshape(k_count, both, -1)
    pairs = both // 2
    left_re = re_side[:, :pairs] + im_side[:, pairs:]
    left_im = im_side[:, :pairs] - re_side[:, pairs:]
    return jnp.concatenate([left_re, left_im], axis=1)


def times_matched(left, matched):
    high_part = left.astype(jnp.bfloat16)
    low_part = (left - high_part.astype(jnp.float32)).astype(jnp.bfloat16)
    rows = left.shape[0]
    both_parts = jnp.concatenate([high_part, low_part], axis=0)
    dims = (((1,), (1,)), ((), ()))
    added = lax.dot_general(both_parts, matched, dims, preferred_element_type=jnp.float32)
    return added[:rows] + added[rows:]


def first_kernel(flags, *refs, first_slot, n_slots, columns, places, leads, turns, step):
    n_chunks = len(columns)
    w_refs = [refs[5 * i : 5 * i + 5] for i in range(n_chunks)]
    rest = refs[5 * n_chunks :]
    of_end, of_mid = rest[:n_slots], rest[n_slots : 2 * n_slots]
    left, flags_out, w_buf, m_buf, out_buf, w_sems, m_sems, out_sems = rest[2 * n_slots :]
    depth = w_buf.shape[1]
    _, k_count, both, _ = m_buf.shape
    copies, used = [], 0
    for i in range(n_chunks):
        for at in range(0, columns[i][1], step):
            copies.append(w_copies(w_refs[i], places[i], turns, w_buf, at, used, step, w_sems.at[used // step]))
            used += step
    total = used // step
    for copy in copies[0]:
        copy.start()
    for s in range(n_slots):
        end_part, mid_part = part_of(of_end[s], leads[s], k_count), part_of(of_mid[s], leads[n_slots + s], k_count)
        m_copies(flags, turns, end_part, mid_part, m_buf.at[s], m_sems.at[s])
    for here in copies[1:]:
        for copy in here:
            copy.start()
    keep_flags(flags, flags_out)

    def out_copy(t):
        start = pl.multiple_of(t * step, STEP)
        target = left.at[:, :, :, pl.ds(start, step)]
        return pltpu.make_async_copy(out_buf.at[t % 2], target, out_sems.at[t % 2])

    def one_step(t, carry):
        @pl.when(t >= 2)
        def _():
            out_copy(t - 2).wait()

        for copy in w_copies(w_refs[0], places[0], turns, w_buf, 0, 0, step, w_sems.at[t]):
            copy.wait()
        for s in range(n_slots):
            @pl.when(t == 0)
            def _():
                pltpu.make_async_copy(m_buf.at[s], m_buf.at[s], m_sems.at[s]).wait()

        for at in range(0, step, STEP):
            start = pl.multiple_of(t * step + at, STEP)
            for s in range(n_slots):
                lhs = m_buf[s].reshape(k_count * both, depth)
                w_re, w_im = w_buf[0, :, pl.ds(start, STEP)], w_buf[1, :, pl.ds(start, STEP)]
                out_buf[t % 2, s, :, :, at : at + STEP] = left_tile(lhs, w_re, w_im, k_count, both)
        out_copy(t).start()
        return carry

    lax.fori_loop(0, total, one_step, 0)
    for t in range(max(total - 2, 0), total):
        out_copy(t).wait()


def first_product(flags, chunks, turns, first_slot, n_slots, of_end, of_mid):
    depth = len(turns) * chunks[0][2][0].shape[0]
    both, k_count = of_end[first_slot][0].shape[1], 4
    columns = tuple((first, width) for first, width, _, _ in chunks)
    span = sum(width for _, width in columns)
    slots = range(first_slot, first_slot + n_slots)
    step = WIDE_STEP if n_slots == 1 and all(width % WIDE_STEP == 0 for _, width in columns) else STEP
    chosen = [of_end[s] for s in slots] + [of_mid[s] for s in slots]
    operands = [ref for _, _, blocks, _ in chunks for ref in blocks] + [ref for ref, _ in chosen]
    return pl.pallas_call(
        functools.partial(
            first_kernel,
            first_slot=first_slot,
            n_slots=n_slots,
            columns=columns,
            places=tuple(places for _, _, _, places in chunks),
            leads=tuple(lead for _, lead in chosen),
            turns=turns,
            step=step,
        ),
        out_shape=(jax.ShapeDtypeStruct((n_slots, k_count, both, span), jnp.float32), FLAGS),
        in_specs=[IN_SMEM] + [ANYWHERE] * len(operands),
        out_specs=(ANYWHERE, IN_SMEM),
        scratch_shapes=[
            pltpu.VMEM((2, depth, span), jnp.bfloat16),
            pltpu.VMEM((n_slots, k_count, both, depth), jnp.bfloat16),
            pltpu.VMEM((2, n_slots, k_count, both, step), jnp.float32),
            pltpu.SemaphoreType.DMA((span // step, 8)),
            pltpu.SemaphoreType.DMA((n_slots,)),
            pltpu.SemaphoreType.DMA((2,)),
        ],
        compiler_params=PARAMS,
        cost_estimate=COST,
        name="first_product",
    )(flags, *operands)


def second_kernel(flags, *refs, n_lefts, leads, base, width):
    lefts, matched = refs[:n_lefts], refs[n_lefts : n_lefts + 8]
    sums, flags_out, left_buf, c_buf, left_sems, c_sems = refs[n_lefts + 8 :]
    n_slots, k_count = c_buf.shape[:2]

    def left_start(t):
        s, k, at = t // k_count, t % k_count, 0
        for left in lefts:
            here = s - at

            @pl.when((here >= 0) & (here < left.shape[0]))
            def _():
                pltpu.make_async_copy(left.at[here, k], left_buf.at[t % 4], left_sems.at[t % 4]).start()

            at += left.shape[0]

    for t in range(4):
        left_start(t)
    matched_copies(flags, matched, leads, c_buf, 0, base, width, c_sems)
    keep_flags(flags, flags_out)

    def step(t, carry):
        s, k = t // k_count, t % k_count

        @pl.when(k == 0)
        def _():
            matched_wait(c_buf, s, c_sems)

        pltpu.make_async_copy(lefts[0].at[0, 0], left_buf.at[t % 4], left_sems.at[t % 4]).wait()
        sums[s, k] = times_matched(left_buf[t % 4], c_buf[s, (k + flags[3]) % k_count])

        @pl.when(t + 4 < n_slots * k_count)
        def _():
            left_start(t + 4)

        return carry

    lax.fori_loop(0, n_slots * k_count, step, 0)


def second_product(flags, lefts, matched, base, width):
    n_slots = sum(left.shape[0] for left in lefts)
    _, k_count, both, _ = lefts[0].shape
    return pl.pallas_call(
        functools.partial(
            second_kernel, n_lefts=len(lefts), leads=tuple(lead for _, lead in matched), base=base, width=width
        ),
        out_shape=(jax.ShapeDtypeStruct((n_slots, k_count, both, both), jnp.float32), FLAGS),
        in_specs=[IN_SMEM] + [ANYWHERE] * (len(lefts) + len(matched)),
        out_specs=(IN_VMEM, IN_SMEM),
        scratch_shapes=[
            pltpu.VMEM((4, both, width), jnp.float32),
            pltpu.VMEM((n_slots, k_count, both, width), jnp.bfloat16),
            pltpu.SemaphoreType.DMA((4,)),
            pltpu.SemaphoreType.DMA((n_slots,)),
        ],
        compiler_params=PARAMS,
        cost_estimate=COST,
        name="second_product",
    )(flags, *lefts, *[ref for ref, _ in matched])


def both_kernel(flags, *refs, first_slot, n_slots, columns, places, leads, turns, sums_at, stored, last):
    n_chunks = len(columns)
    w_refs = [refs[5 * i : 5 * i + 5] for i in range(n_chunks)]
    rest = refs[5 * n_chunks :]
    of_end, of_mid, rest = rest[:n_slots], rest[n_slots : 2 * n_slots], rest[2 * n_slots :]
    matched, rest = rest[:8], rest[8:]
    sums_in, rest = rest[: len(sums_at)], rest[len(sums_at) :]
    if stored:
        left, rest = rest[0], rest[1:]
    sums, flags_out, w_buf, m_buf, c_buf, left_buf, acc, w_sems, m_sems, c_sems, left_sems = rest
    depth, span = w_buf.shape[1:]
    _, k_count, both, _ = m_buf.shape
    n_tiles = span // STEP
    copies, used = [], 0
    for i in range(n_chunks):
        for at in range(0, columns[i][1], STEP):
            copies.append(w_copies(w_refs[i], places[i], turns, w_buf, at, used, STEP, w_sems.at[used // STEP]))
            used += STEP
    for copy in copies[0]:
        copy.start()

    def left_copy(s):
        return pltpu.make_async_copy(left.at[s], left_buf.at[s % 2], left_sems.at[s % 2])

    for s in range(n_slots):
        end_part, mid_part = part_of(of_end[s], leads[s], k_count), part_of(of_mid[s], leads[n_slots + s], k_count)
        m_copies(flags, turns, end_part, mid_part, m_buf.at[s], m_sems.at[s])
        if s == 0 and stored:
            left_copy(0).start()
    for here in copies[1:]:
        for copy in here:
            copy.start()
    matched_copies(flags, matched, leads[2 * n_slots :], c_buf, first_slot, columns[0][0], span, c_sems)
    keep_flags(flags, flags_out)
    acc[...] = jnp.zeros(acc.shape, acc.dtype)
    for at, one in zip(sums_at, sums_in):
        count = one.shape[0]
        acc[at : at + count] = acc[at : at + count] + one[...]

    def one_step(t, carry):
        s, tile_number = t // n_tiles, t % n_tiles
        start = pl.multiple_of(tile_number * STEP, STEP)

        @pl.when(s == 0)
        def _():
            for copy in w_copies(w_refs[0], places[0], turns, w_buf, 0, 0, STEP, w_sems.at[tile_number]):
                copy.wait()

        @pl.when(tile_number == 0)
        def _():
            pltpu.make_async_copy(m_buf.at[s], m_buf.at[s], m_sems.at[s]).wait()
            if stored:
                left_copy(s).wait()

                @pl.when(s + 1 < n_slots)
                def _():
                    left_copy(s + 1).start()

        lhs = m_buf[s].reshape(k_count * both, depth)
        tile = left_tile(lhs, w_buf[0, :, pl.ds(start, STEP)], w_buf[1, :, pl.ds(start, STEP)], k_count, both)
        if stored:
            tile = tile + left_buf[s % 2, :, :, pl.ds(start, STEP)]
        left_buf[s % 2, :, :, pl.ds(start, STEP)] = tile

        @pl.when(tile_number == n_tiles - 1)
        def _():
            matched_wait(c_buf, s, c_sems)
            for k in range(k_count):
                acc[s, k] = acc[s, k] + times_matched(left_buf[s % 2, k], c_buf[s, (k + flags[3]) % k_count])

        return carry

    lax.fori_loop(0, n_slots * n_tiles, one_step, 0)
    if last:
        pairs = both // 2
        sums[:, :, :, :pairs] = acc[:, :, :pairs, :pairs] - acc[:, :, pairs:, pairs:]
        sums[:, :, :, pairs:] = acc[:, :, :pairs, pairs:] + acc[:, :, pairs:, :pairs]
    else:
        sums[...] = acc[...]


def both_products(flags, chunks, turns, first_slot, n_slots, of_end, of_mid, matched, sums=(), left=None, last=False):
    k_count = 4
    both = of_end[0][0].shape[1]
    depth = len(turns) * chunks[0][2][0].shape[0]
    columns = tuple((first, width) for first, width, _, _ in chunks)
    span = sum(width for _, width in columns)
    slots = range(first_slot, first_slot + n_slots)
    chosen = [of_end[s] for s in slots] + [of_mid[s] for s in slots] + list(matched)
    operands = [ref for _, _, blocks, _ in chunks for ref in blocks] + [ref for ref, _ in chosen]
    stored = [] if left is None else [left]
    return pl.pallas_call(
        functools.partial(
            both_kernel,
            first_slot=first_slot,
            n_slots=n_slots,
            columns=columns,
            places=tuple(places for _, _, _, places in chunks),
            leads=tuple(lead for _, lead in chosen),
            turns=turns,
            sums_at=tuple(at for at, _ in sums),
            stored=left is not None,
            last=last,
        ),
        out_shape=(jax.ShapeDtypeStruct((n_slots, k_count, both // 2 if last else both, both), jnp.float32), FLAGS),
        in_specs=[IN_SMEM] + [ANYWHERE] * len(operands) + [IN_VMEM] * len(sums) + [ANYWHERE] * len(stored),
        out_specs=(IN_VMEM, IN_SMEM),
        scratch_shapes=[
            pltpu.VMEM((2, depth, span), jnp.bfloat16),
            pltpu.VMEM((n_slots, k_count, both, depth), jnp.bfloat16),
            pltpu.VMEM((n_slots, k_count, both, span), jnp.bfloat16),
            pltpu.VMEM((2, k_count, both, span), jnp.float32),
            pltpu.VMEM((n_slots, k_count, both, both), jnp.float32),
            pltpu.SemaphoreType.DMA((span // STEP, 8)),
            pltpu.SemaphoreType.DMA((n_slots,)),
            pltpu.SemaphoreType.DMA((n_slots,)),
            pltpu.SemaphoreType.DMA((2,)),
        ],
        compiler_params=PARAMS,
        cost_estimate=COST,
        name="both_products",
    )(flags, *operands, *[one for _, one in sums], *stored)


def turn_kernel(flags, first, second, first_turned, second_turned, turned_pair):
    first_turned[0] = first[0].T
    second_turned[0] = second[0].T
    turned_pair[0, 0] = second_turned[0]
    turned_pair[1, 0] = first_turned[0]


def turned_parts(flags, densities):
    k_count, n_rows, both = densities.shape
    quarter = n_rows // 4

    def part(which):
        return pl.BlockSpec((1, quarter, both), lambda k, flags: (k, flags[which], 0))

    one = pl.BlockSpec((1, both, quarter), lambda k, flags: (k, 0, 0))
    first, second, both_parts = pl.pallas_call(
        turn_kernel,
        out_shape=(
            jax.ShapeDtypeStruct((k_count, both, quarter), densities.dtype),
            jax.ShapeDtypeStruct((k_count, both, quarter), densities.dtype),
            jax.ShapeDtypeStruct((2, k_count, both, quarter), densities.dtype),
        ),
        grid_spec=pltpu.PrefetchScalarGridSpec(
            num_scalar_prefetch=1,
            grid=(k_count,),
            in_specs=[part(6), part(7)],
            out_specs=[
                one,
                one,
                pl.BlockSpec((2, 1, both, quarter), lambda k, flags: (0, k, 0, 0)),
            ],
        ),
        compiler_params=PARAMS,
        cost_estimate=COST,
        name="turned_parts",
    )(flags, densities, densities)
    return first, second, both_parts.reshape(2 * k_count, both, quarter)


def body(densities, screened, partner, pair_order):
    k_count, n_rows, both = densities.shape
    pair_count = both // 2
    quarter = n_rows // 4
    panel = screened.shape[2]
    widths = (panel // 2, panel // 4, panel // 4)
    firsts = [sum(widths[:n]) for n in range(3)]
    k_owner = lax.axis_index("ka")
    c = lax.axis_index("ga")
    z, b = k_owner // 4, k_owner % 4
    half, odd = z // 2, z % 2
    offset = partner[0] % k_count
    ends = (z == 0) | (z == 3)
    flags = jnp.stack([b, c == odd, half, offset, ends, c, 2 * (1 - odd) + c, 2 * odd + c]).astype(jnp.int32)
    rows = screened.shape[1]

    part = (k_count, both, quarter)

    def own_pieces(n, when, at=0):
        first, width = firsts[n], widths[n]
        return [
            (when, screened, real(first, width), columns_of(at, width)),
            (when, screened, imaginary(first, width), columns_of(at + width, width)),
        ]

    def far_part(*numbers):
        pieces, at = [], 0
        for n in numbers:
            pieces += own_pieces(n, own_far, at)
            at += 2 * widths[n]
        return (rows, at), pieces

    def sent_far(value):
        return moved(value, lambda z, b, c: (z ^ 1, b, 1 - c) if c != z % 2 else None)

    def panel_parts(n, arrived, at=0, before=None):
        copies = 0 if before is None else 1
        pieces = [piece + (copies,) for piece in own_pieces(n, own_near)]
        pieces.append((own_far, arrived, columns_of(at, 2 * widths[n]), columns_of(0, 2 * widths[n]), copies))
        if before is None:
            return (((rows, 2 * widths[n]), pieces),)
        x_side, y_side = before
        passed = widths[n - 1]
        shape, place = (rows, 2 * widths[n] + passed), columns_of(2 * widths[n], passed)
        return (
            (shape, pieces + [(always, y_side, columns_of(passed, passed), place)]),
            (shape, [(always, x_side, columns_of(0, passed), place)]),
        )

    first_part, second_part = slots_from(0, k_count), slots_from(k_count, k_count)

    flags, sent_0, sent_1 = moves(flags, (), far_part(0), far_part(1))
    arrived_0, arrived_1 = sent_far(sent_0), sent_far(sent_1)
    own_first, own_second, own_both = turned_parts(flags, densities)
    swapped_0 = other_core(own_second)
    pair_a, mid_ad = end_with_mid(own_first), mid_with_mid(own_both)

    flags, panel_0, sent_2 = moves(flags, (swapped_0,), *panel_parts(0, arrived_0), far_part(2))
    x_0, y_0 = along_x(panel_0), along_y(panel_0)

    flags, to_pair, to_mid = moves(
        flags,
        (),
        (part, [(at_end, own_second, whole, whole), (at_mid, mid_ad, first_part, whole)]),
        (part, [(always, pair_a, whole, whole)]),
    )
    pair_b, mid_b = end_with_mid(to_pair), mid_with_mid(to_mid)

    flags, to_x, to_y, sent_2 = moves(flags, (), *panel_parts(1, arrived_1, 0, (x_0, y_0)), passing=(sent_2,))
    x_1, y_1 = along_x(to_x), along_y(to_y)
    panel_1 = to_x
    arrived_2 = sent_far(sent_2)

    flags, pair_a, pair_b, mid_b = moves(flags, (arrived_2,), passing=(pair_a, pair_b, mid_b))
    swapped_a = other_core(pair_a)
    pair_c, mid_c = mid_to_end(mid_b), mid_with_mid(pair_b)
    of_end = [(own_second, 0), (pair_a, 0), (pair_b, 0), None]
    of_mid = [(own_first, 0), (mid_ad, 0), (mid_b, 0), (pair_b, 0)]
    every = (0, 1, 2, 3)

    flags, to_x, to_y = moves(flags, (), *panel_parts(2, arrived_2, 0, (x_1, y_1)))
    x_2, y_2 = along_x(to_x), along_y(to_y)
    panel_2 = to_x
    chunk_0 = (firsts[0], widths[0], (panel_0, x_0, y_0, y_1, x_1), (widths[0], 2 * widths[1], 2 * widths[1]))
    left_0, flags = first_product(flags, [chunk_0], every, 0, 3, of_end, of_mid)

    flags, late_1, late_2 = moves(
        flags,
        (swapped_a,),
        (part, [(at_end, pair_b, whole, whole), (at_mid, mid_ad, second_part, whole)]),
        (part, [(at_end, pair_c, whole, whole), (at_mid, mid_c, whole, whole)]),
    )
    swapped_1, swapped_2 = other_core(late_1), other_core(late_2)
    of_end[3] = (pair_c, 0)
    matched = [(own_second, 0), (swapped_0, 0), (pair_a, 0), (swapped_a, 0)]
    matched += [(late_1, 0), (swapped_1, 0), (late_2, 0), (swapped_2, 0)]
    left_3, flags = first_product(flags, [chunk_0], every, 3, 1, of_end, of_mid)
    sums_0, flags = second_product(flags, [left_0, left_3], matched, firsts[0], widths[0])

    shape = (rows, widths[2])
    flags, to_x, to_y = moves(
        flags,
        (),
        (shape, [(always, y_2, columns_of(widths[2], widths[2]), whole)]),
        (shape, [(always, x_2, columns_of(0, widths[2]), whole)]),
    )
    x_3, y_3 = along_x(to_x), along_y(to_y)
    chunk_1 = (firsts[1], widths[1], (panel_1, x_1, y_1, y_2, x_2), (widths[1], 2 * widths[2], 2 * widths[2]))
    sums_1, flags = both_products(flags, [chunk_1], every, 0, 4, of_end, of_mid, matched, sums=((0, sums_0),))
    chunk_2 = (firsts[2], widths[2], (panel_2, x_2, y_2, y_3, x_3), (widths[2], 0, 0))
    blocks, flags = both_products(
        flags, [chunk_2], every, 0, 4, of_end, of_mid, matched, sums=((0, sums_1),), last=True
    )

    pairs_of_k = k_count // 2
    mine = lax.dynamic_slice_in_dim(blocks, c * pairs_of_k, pairs_of_k, 1)
    mine = mine + other_core(lax.dynamic_slice_in_dim(blocks, (1 - c) * pairs_of_k, pairs_of_k, 1))
    up_order = jnp.where(half == 0, mine, jnp.stack([mine[0], mine[3], mine[2], mine[1]]))
    total = jnp.stack([up_order[0], up_order[3]])
    for shift in (1, 2, 3):
        sent = jnp.stack([up_order[shift], up_order[shift - 1]])
        total = total + moved(sent, lambda z, b, c: ((z + shift) % 4, b, c))
    theirs = other_core(total)
    total = jnp.where(c == 0, jnp.concatenate([total, theirs], axis=1), jnp.concatenate([theirs, total], axis=1))
    total = total.reshape(2 * k_count, pair_count, both)
    order_table = (jnp.arange(pair_count)[:, None] == pair_order[None, :]).astype(jnp.float32)
    filed = reorder(total[:, :, :pair_count], total[:, :, pair_count:], order_table)
    sources = (jnp.arange(k_count) - offset) % k_count
    mirror = conjugate_side(jnp.take(filed[k_count:], sources, axis=0), pair_count)
    return (filed[:k_count], mirror)


def solution(mesh):
    in_specs = (P("ka", None, None), P(None, "ka", "ga"), P(), P())
    out_specs = (P("ka", None, None), P("ka", None, None))
    planes = mesh.shape["ka"] == 16 and mesh.shape["ga"] == 2
    chosen = body if planes else general_body
    return jax.shard_map(chosen, mesh=mesh, in_specs=in_specs, out_specs=out_specs, check_vma=False)
```

```python
import functools

import jax
import jax.numpy as jnp
from jax import lax
from jax.experimental import pallas as pl
from jax.experimental.pallas import tpu as pltpu
from jax.sharding import PartitionSpec as P


def passed_along(value, axis, steps):
    count = lax.axis_size(axis)
    pairs = [(source, (source + steps) % count) for source in range(count)]
    return lax.ppermute(value, axis, pairs)


def conjugate_side(blocks, pair_count):
    real_half = jnp.swapaxes(blocks[:, :, :pair_count], 1, 2)
    imag_half = jnp.swapaxes(blocks[:, :, pair_count:], 1, 2)
    return jnp.concatenate([real_half, -imag_half], axis=2)


def combine_terms(partial_value, order_table, pair_count):
    block_re = partial_value[:, 0, :, :pair_count] - partial_value[:, 1, :, pair_count:]
    block_im = partial_value[:, 0, :, pair_count:] + partial_value[:, 1, :, :pair_count]
    return reorder(block_re, block_im, order_table)


def reorder(block_re, block_im, order_table):
    block_re = jnp.einsum("kpq,qj->kpj", block_re, order_table, precision=lax.Precision.HIGHEST)
    block_im = jnp.einsum("kpq,qj->kpj", block_im, order_table, precision=lax.Precision.HIGHEST)
    return jnp.concatenate([block_re, block_im], axis=2)


def finish_terms(left_sums, matched, pair_count):
    left_re = left_sums[:, 0, :pair_count] + left_sums[:, 1, pair_count:]
    left_im = left_sums[:, 1, :pair_count] - left_sums[:, 0, pair_count:]
    left_factor = jnp.stack([left_re, left_im], axis=1)
    return jnp.einsum(
        "kwpc,kcq->kwpq", left_factor, matched.astype(jnp.float32), precision=lax.Precision.HIGHEST
    )


def general_body(densities, screened, partner, pair_order):
    k_count = densities.shape[0]
    pair_count = densities.shape[2] // 2
    panel_width = screened.shape[2]
    k_owner = lax.axis_index("ka")
    column = lax.axis_index("ga")
    own_columns = lax.dynamic_slice_in_dim(densities, column * panel_width, panel_width, 1)
    arrived = passed_along(own_columns, "ka", -4)
    own_partner = lax.dynamic_slice_in_dim(partner, k_owner * k_count, k_count, 0)
    slot_index = own_partner % k_count
    offset = slot_index[0]
    matched = jnp.take(arrived, slot_index, axis=0)
    left_sums = jnp.einsum(
        "kgp,wgc->kwpc",
        densities,
        lax.all_gather(screened, "ka", axis=1, tiled=True),
        preferred_element_type=jnp.float32,
    )
    partial_value = finish_terms(left_sums, matched, pair_count)
    order_table = (jnp.arange(pair_count)[:, None] == pair_order[None, :]).astype(jnp.float32)
    sources = (jnp.arange(k_count) - offset) % k_count
    summed = lax.psum(partial_value, "ga")
    direct = combine_terms(summed, order_table, pair_count)
    received = passed_along(direct, "ka", 4)
    mirror = conjugate_side(jnp.take(received, sources, axis=0), pair_count)
    return (direct, mirror)


AXES = ("ka", "ga")
STEP = 256
WIDE_STEP = 512


def device(z, b, c):
    return (z * 4 + b) * 2 + c


def moved(value, rule):
    pairs = []
    for z in range(4):
        for b in range(4):
            for c in range(2):
                target = rule(z, b, c)
                if target is not None:
                    pairs.append((device(z, b, c), device(*target)))
    return lax.ppermute(value, AXES, pairs)


def along_x(value):
    return moved(value, lambda z, b, c: (z, b ^ 1, c))


def along_y(value):
    return moved(value, lambda z, b, c: (z, b ^ 2, c))


def other_core(value):
    return moved(value, lambda z, b, c: (z, b, 1 - c))


def end_with_mid(value):
    return moved(value, lambda z, b, c: (z ^ 1, b, c))


def mid_to_end(value):
    return moved(value, lambda z, b, c: (z ^ 1, b, c) if z in (1, 2) else None)


def mid_with_mid(value):
    return moved(value, lambda z, b, c: (3 - z, b, c) if z in (1, 2) else None)


ANYWHERE = pl.BlockSpec(memory_space=pltpu.HBM)
IN_SMEM = pl.BlockSpec(memory_space=pltpu.SMEM)
IN_VMEM = pl.BlockSpec(memory_space=pltpu.VMEM)
PARAMS = pltpu.CompilerParams(vmem_limit_bytes=64 * 1024 * 1024)
COST = pl.CostEstimate(flops=1000, bytes_accessed=1000, transcendentals=0)
FLAGS = jax.ShapeDtypeStruct((8,), jnp.int32)


def keep_flags(flags, out):
    for i in range(flags.shape[0]):
        out[i] = flags[i]


def always(flags):
    return None


def at_end(flags):
    return flags[4] == 1


def at_mid(flags):
    return flags[4] == 0


def own_near(flags):
    return flags[1] == 1


def own_far(flags):
    return flags[1] == 0


def whole(ref):
    return ref


def real(first, width):
    return lambda ref: ref.at[0, :, first : first + width]


def imaginary(first, width):
    return lambda ref: ref.at[1, :, first : first + width]


def columns_of(first, width):
    return lambda ref: ref.at[:, first : first + width]


def slots_from(first, count):
    return lambda ref: ref.at[first : first + count]


def moves_kernel(flags, *refs, plan, n_sources, n_outs, n_passing):
    sources, outs = refs[:n_sources], refs[n_sources : n_sources + n_outs]
    flags_out, *stages = refs[n_sources + n_outs + n_passing : -2]
    in_sems, out_sems = refs[-2:]

    def run(chosen, act):
        if chosen is None:
            act()
        else:
            pl.when(chosen)(act)

    copies = []
    for i, (when, number, view, out_numbers, target) in enumerate(plan):
        stage = target(stages[out_numbers[0]])
        load = pltpu.make_async_copy(view(sources[number]), stage, in_sems.at[i])
        stores = [
            pltpu.make_async_copy(stage, target(outs[out_number]), out_sems.at[i, j])
            for j, out_number in enumerate(out_numbers)
        ]
        copies.append((when(flags), load, stores))
        run(when(flags), load.start)
    keep_flags(flags, flags_out)
    for chosen, load, stores in copies:
        def forward():
            load.wait()
            for store in stores:
                store.start()

        run(chosen, forward)
    for chosen, _, stores in copies:
        for store in stores:
            run(chosen, store.wait)


def moves(flags, waits, *outputs, passing=()):
    sources, plan = [], []
    for number, (_, pieces) in enumerate(outputs):
        for when, source, view, target, *more in pieces:
            plan.append((when, len(sources), view, tuple(range(number, number + 1 + sum(more))), target))
            sources.append(source)
    operands = sources + list(waits)
    shapes = [jax.ShapeDtypeStruct(shape, jnp.bfloat16) for shape, _ in outputs]
    aliases = {1 + len(operands) + i: len(outputs) + i for i in range(len(passing))}
    operands += list(passing)
    shapes += [jax.ShapeDtypeStruct(value.shape, value.dtype) for value in passing]
    results = pl.pallas_call(
        functools.partial(
            moves_kernel, plan=tuple(plan), n_sources=len(operands), n_outs=len(outputs), n_passing=len(passing)
        ),
        out_shape=tuple(shapes) + (FLAGS,),
        in_specs=[IN_SMEM] + [ANYWHERE] * len(operands),
        out_specs=(ANYWHERE,) * len(shapes) + (IN_SMEM,),
        input_output_aliases=aliases,
        scratch_shapes=[pltpu.VMEM(shape, jnp.bfloat16) for shape, _ in outputs]
        + [pltpu.SemaphoreType.DMA((max(len(plan), 1),)), pltpu.SemaphoreType.DMA((max(len(plan), 1), 2))],
        compiler_params=PARAMS,
        cost_estimate=COST,
        name="moves",
    )(flags, *operands)
    return results[-1], *results[:-1]


def w_copies(blocks, places, turns, w_buf, source_at, target_at, step, sems):
    width, real_at, imaginary_at = places
    rows = w_buf.shape[1] // len(turns)
    copies = []
    for i, turn in enumerate(turns):
        for part in range(2):
            source = blocks[turn] if turn < 3 else blocks[3 + part]
            first = (real_at, imaginary_at)[part] if turn == 3 else part * width
            target = w_buf.at[part, i * rows : (i + 1) * rows, target_at : target_at + step]
            source = source.at[:, first + source_at : first + source_at + step]
            copies.append(pltpu.make_async_copy(source, target, sems.at[len(copies)]))
    return copies


def m_copies(flags, turns, end_part, mid_part, target, sem):
    rows = target.shape[2] // len(turns)
    for i, turn in enumerate(turns):
        start = pl.multiple_of((flags[0] ^ turn) * rows, rows)
        window = pl.ds(start, rows)
        place = target.at[:, :, i * rows : (i + 1) * rows]
        either(at_end(flags), end_part.at[:, :, window], mid_part.at[:, :, window], place, sem)


def part_of(ref, lead, count):
    return ref.at[lead : lead + count]


def either(chosen, first, second, target, sem):
    a = pltpu.make_async_copy(first, target, sem)
    b = pltpu.make_async_copy(second, target, sem)
    pl.when(chosen)(a.start)
    pl.when(jnp.logical_not(chosen))(b.start)
    return a


def matched_copies(flags, matched, leads, c_buf, slots, first, width, sems, first_slot=0):
    k_count = c_buf.shape[1]
    pairs = [[part_of(matched[2 * i + j], leads[2 * i + j], k_count) for j in range(2)] for i in range(4)]
    quarter = matched[0].shape[2]
    for s in slots:
        for half, s_matched in ((0, (first_slot + s + 1) % 4), (1, (first_slot + s - 1) % 4)):
            for end, order in ((1, (0, 1, 2, 3)), (0, (0, 2, 3, 1))):
                for number in range(2):
                    low, high = max(first, number * quarter), min(first + width, (number + 1) * quarter)
                    if low >= high:
                        continue
                    for core in range(2):
                        source = pairs[order[s_matched]][0 if core == number else 1]
                        copy = pltpu.make_async_copy(
                            source.at[:, :, low - number * quarter : high - number * quarter],
                            c_buf.at[s, :, :, low - first : high - first],
                            sems.at[s],
                        )
                        pl.when((flags[2] == half) & (flags[4] == end) & (flags[5] == core))(copy.start)


def matched_wait(c_buf, s, sems):
    pltpu.make_async_copy(c_buf.at[s], c_buf.at[s], sems.at[s]).wait()


def left_tile(lhs, w_re, w_im, k_count, both):
    re_side = jnp.dot(lhs, w_re, preferred_element_type=jnp.float32).reshape(k_count, both, -1)
    im_side = jnp.dot(lhs, w_im, preferred_element_type=jnp.float32).reshape(k_count, both, -1)
    pairs = both // 2
    left_re = re_side[:, :pairs] + im_side[:, pairs:]
    left_im = im_side[:, :pairs] - re_side[:, pairs:]
    return jnp.concatenate([left_re, left_im], axis=1)


def times_matched(left, matched):
    high_part = left.astype(jnp.bfloat16)
    low_part = (left - high_part.astype(jnp.float32)).astype(jnp.bfloat16)
    rows = left.shape[0]
    both_parts = jnp.concatenate([high_part, low_part], axis=0)
    dims = (((1,), (1,)), ((), ()))
    added = lax.dot_general(both_parts, matched, dims, preferred_element_type=jnp.float32)
    return added[:rows] + added[rows:]


def first_kernel(flags, *refs, first_slot, n_slots, columns, places, leads, turns, step):
    n_chunks = len(columns)
    w_refs = [refs[5 * i : 5 * i + 5] for i in range(n_chunks)]
    rest = refs[5 * n_chunks :]
    of_end, of_mid = rest[:n_slots], rest[n_slots : 2 * n_slots]
    left, flags_out, w_buf, m_buf, out_buf, w_sems, m_sems, out_sems = rest[2 * n_slots :]
    depth = w_buf.shape[1]
    _, k_count, both, _ = m_buf.shape
    copies, used = [], 0
    for i in range(n_chunks):
        for at in range(0, columns[i][1], step):
            copies.append(w_copies(w_refs[i], places[i], turns, w_buf, at, used, step, w_sems.at[used // step]))
            used += step
    total = used // step
    for s in range(max(n_slots, len(copies))):
        if s < len(copies):
            for copy in copies[s]:
                copy.start()
        if s < n_slots:
            end_part, mid_part = part_of(of_end[s], leads[s], k_count), part_of(of_mid[s], leads[n_slots + s], k_count)
            m_copies(flags, turns, end_part, mid_part, m_buf.at[s], m_sems.at[s])
    keep_flags(flags, flags_out)

    def out_copy(t):
        start = pl.multiple_of(t * step, STEP)
        target = left.at[:, :, :, pl.ds(start, step)]
        return pltpu.make_async_copy(out_buf.at[t % 2], target, out_sems.at[t % 2])

    def one_step(t, carry):
        @pl.when(t >= 2)
        def _():
            out_copy(t - 2).wait()

        for copy in w_copies(w_refs[0], places[0], turns, w_buf, 0, 0, step, w_sems.at[t]):
            copy.wait()
        @pl.when(t == 0)
        def _():
            for s in range(n_slots):
                pltpu.make_async_copy(m_buf.at[s], m_buf.at[s], m_sems.at[s]).wait()

        for at in range(0, step, STEP):
            start = pl.multiple_of(t * step + at, STEP)
            for s in range(n_slots):
                lhs = m_buf[s].reshape(k_count * both, depth)
                w_re, w_im = w_buf[0, :, pl.ds(start, STEP)], w_buf[1, :, pl.ds(start, STEP)]
                out_buf[t % 2, s, :, :, at : at + STEP] = left_tile(lhs, w_re, w_im, k_count, both)
        out_copy(t).start()
        return carry

    lax.fori_loop(0, total, one_step, 0)
    for t in range(max(total - 2, 0), total):
        out_copy(t).wait()


def first_product(flags, chunks, turns, first_slot, n_slots, of_end, of_mid):
    depth = len(turns) * chunks[0][2][0].shape[0]
    both, k_count = of_end[first_slot][0].shape[1], 4
    columns = tuple((first, width) for first, width, _, _ in chunks)
    span = sum(width for _, width in columns)
    slots = range(first_slot, first_slot + n_slots)
    step = WIDE_STEP if n_slots == 1 and all(width % WIDE_STEP == 0 for _, width in columns) else STEP
    chosen = [of_end[s] for s in slots] + [of_mid[s] for s in slots]
    operands = [ref for _, _, blocks, _ in chunks for ref in blocks] + [ref for ref, _ in chosen]
    return pl.pallas_call(
        functools.partial(
            first_kernel,
            first_slot=first_slot,
            n_slots=n_slots,
            columns=columns,
            places=tuple(places for _, _, _, places in chunks),
            leads=tuple(lead for _, lead in chosen),
            turns=turns,
            step=step,
        ),
        out_shape=(jax.ShapeDtypeStruct((n_slots, k_count, both, span), jnp.float32), FLAGS),
        in_specs=[IN_SMEM] + [ANYWHERE] * len(operands),
        out_specs=(ANYWHERE, IN_SMEM),
        scratch_shapes=[
            pltpu.VMEM((2, depth, span), jnp.bfloat16),
            pltpu.VMEM((n_slots, k_count, both, depth), jnp.bfloat16),
            pltpu.VMEM((2, n_slots, k_count, both, step), jnp.float32),
            pltpu.SemaphoreType.DMA((span // step, 8)),
            pltpu.SemaphoreType.DMA((n_slots,)),
            pltpu.SemaphoreType.DMA((2,)),
        ],
        compiler_params=PARAMS,
        cost_estimate=COST,
        name="first_product",
    )(flags, *operands)


def stored_kernel(flags, *refs, n_slots, n_lefts, columns, places, leads):
    first, width = columns
    w_refs, of_end, of_mid = refs[:5], refs[5 : 5 + n_slots], refs[5 + n_slots : 5 + 2 * n_slots]
    matched, rest = refs[5 + 2 * n_slots : 13 + 2 * n_slots], refs[13 + 2 * n_slots :]
    lefts, (sums, flags_out, w_buf, m_buf, c_buf, left_buf, w_sems, m_sems, c_sems, left_sems) = rest[:n_lefts], rest[n_lefts:]
    depth = w_buf.shape[1]
    all_slots, k_count, both, _ = c_buf.shape
    n_tiles = width // STEP
    sources = [left.at[i] for left in lefts for i in range(left.shape[0])]
    w_loads = w_copies(w_refs, places, (3,), w_buf, 0, 0, width, w_sems)
    for copy in w_loads:
        copy.start()
    for s in range(all_slots):
        if s < n_slots:
            end_part, mid_part = part_of(of_end[s], leads[s], k_count), part_of(of_mid[s], leads[n_slots + s], k_count)
            m_copies(flags, (3,), end_part, mid_part, m_buf.at[s], m_sems.at[s])
        pltpu.make_async_copy(sources[s], left_buf.at[s], left_sems.at[s]).start()
        matched_copies(flags, matched, leads[2 * n_slots :], c_buf, (s,), first, width, c_sems)
    keep_flags(flags, flags_out)
    for copy in w_loads:
        copy.wait()

    def second(s):
        matched_wait(c_buf, s, c_sems)
        for k in range(k_count):
            sums[s, k] = times_matched(left_buf[s, k], c_buf[s, (k + flags[3]) % k_count])

    def one_step(t, carry):
        s, tile_number = t // n_tiles, t % n_tiles
        start = pl.multiple_of(tile_number * STEP, STEP)

        @pl.when(tile_number == 0)
        def _():
            pltpu.make_async_copy(m_buf.at[s], m_buf.at[s], m_sems.at[s]).wait()
            pltpu.make_async_copy(left_buf.at[s], left_buf.at[s], left_sems.at[s]).wait()

        lhs = m_buf[s].reshape(k_count * both, depth)
        tile = left_tile(lhs, w_buf[0, :, pl.ds(start, STEP)], w_buf[1, :, pl.ds(start, STEP)], k_count, both)
        left_buf[s, :, :, pl.ds(start, STEP)] = left_buf[s, :, :, pl.ds(start, STEP)] + tile

        @pl.when(tile_number == n_tiles - 1)
        def _():
            second(s)

        return carry

    lax.fori_loop(0, n_slots * n_tiles, one_step, 0)

    def only_second(s, carry):
        pltpu.make_async_copy(left_buf.at[s], left_buf.at[s], left_sems.at[s]).wait()
        second(s)
        return carry

    lax.fori_loop(n_slots, all_slots, only_second, 0)


def stored_products(flags, chunk, of_end, of_mid, matched, lefts):
    n_slots, k_count, both, _ = lefts[0].shape
    all_slots = sum(left.shape[0] for left in lefts)
    first, width, blocks, places = chunk
    rows = blocks[0].shape[0]
    chosen = list(of_end[:n_slots]) + list(of_mid[:n_slots]) + list(matched)
    operands = list(blocks) + [ref for ref, _ in chosen] + list(lefts)
    return pl.pallas_call(
        functools.partial(
            stored_kernel,
            n_slots=n_slots,
            n_lefts=len(lefts),
            columns=(first, width),
            places=places,
            leads=tuple(lead for _, lead in chosen),
        ),
        out_shape=(jax.ShapeDtypeStruct((all_slots, k_count, both, both), jnp.float32), FLAGS),
        in_specs=[IN_SMEM] + [ANYWHERE] * len(operands),
        out_specs=(IN_VMEM, IN_SMEM),
        scratch_shapes=[
            pltpu.VMEM((2, rows, width), jnp.bfloat16),
            pltpu.VMEM((n_slots, k_count, both, rows), jnp.bfloat16),
            pltpu.VMEM((all_slots, k_count, both, width), jnp.bfloat16),
            pltpu.VMEM((all_slots, k_count, both, width), jnp.float32),
            pltpu.SemaphoreType.DMA((2,)),
            pltpu.SemaphoreType.DMA((n_slots,)),
            pltpu.SemaphoreType.DMA((all_slots,)),
            pltpu.SemaphoreType.DMA((all_slots,)),
        ],
        compiler_params=PARAMS,
        cost_estimate=COST,
        name="stored_products",
    )(flags, *operands)


def both_kernel(flags, *refs, n_slots, columns, places, leads):
    n_chunks = len(columns)
    first = columns[0][0]
    w_refs, rest = [refs[5 * i : 5 * i + 5] for i in range(n_chunks)], refs[5 * n_chunks :]
    of_end, of_mid, rest = rest[:n_slots], rest[n_slots : 2 * n_slots], rest[2 * n_slots :]
    matched, sums_in, kept, given = rest[:8], rest[8], rest[9], rest[10]
    w_buf, m_buf, c_buf, left_buf, acc, w_sems, m_sems, c_sems, sums_sem = rest[11:]
    depth, span = w_buf.shape[1:]
    _, k_count, both, _ = m_buf.shape
    n_tiles = span // STEP
    turns = (0, 1, 2, 3)

    tiles = [(i, at) for i in range(n_chunks) for at in range(0, columns[i][1], STEP)]

    def w_tile(number):
        i, at = tiles[number]
        return w_copies(w_refs[i], places[i], turns, w_buf, at, number * STEP, STEP, w_sems.at[number])

    def m_start(s):
        end_part, mid_part = part_of(of_end[s], leads[s], k_count), part_of(of_mid[s], leads[n_slots + s], k_count)
        m_copies(flags, turns, end_part, mid_part, m_buf.at[s], m_sems.at[s])

    def c_start(s):
        matched_copies(flags, matched, leads[2 * n_slots :], c_buf, (s,), first, span, c_sems)

    for copy in w_tile(0):
        copy.start()
    m_start(0)
    for i in range(1, n_tiles):
        for copy in w_tile(i):
            copy.start()
    m_start(1)
    c_start(0)
    sums_copy = pltpu.make_async_copy(sums_in, acc, sums_sem)
    sums_copy.start()

    def one_step(t, carry):
        s, tile_number = t // n_tiles, t % n_tiles
        start = pl.multiple_of(tile_number * STEP, STEP)

        @pl.when(s == 0)
        def _():
            for copy in w_copies(w_refs[0], places[0], turns, w_buf, 0, 0, STEP, w_sems.at[tile_number]):
                copy.wait()

        @pl.when(tile_number == 0)
        def _():
            pltpu.make_async_copy(m_buf.at[s], m_buf.at[s], m_sems.at[s]).wait()

        for j in range(n_slots - 1):
            @pl.when(t == j * n_tiles)
            def _():
                if j + 2 < n_slots:
                    m_start(j + 2)
                c_start(j + 1)

        lhs = m_buf[s].reshape(k_count * both, depth)
        tile = left_tile(lhs, w_buf[0, :, pl.ds(start, STEP)], w_buf[1, :, pl.ds(start, STEP)], k_count, both)
        left_buf[:, :, pl.ds(start, STEP)] = tile

        @pl.when(t == n_tiles - 1)
        def _():
            sums_copy.wait()

        @pl.when(tile_number == n_tiles - 1)
        def _():
            matched_wait(c_buf, s, c_sems)
            for k in range(k_count):
                acc[s, k] = acc[s, k] + times_matched(left_buf[k], c_buf[s, (k + flags[3]) % k_count])

        return carry

    lax.fori_loop(0, n_slots * n_tiles, one_step, 0)
    pairs, own_k = both // 2, k_count // 2
    for s in range(n_slots):
        above = jnp.where(flags[2] == 0, s, (n_slots - s) % n_slots)
        for k in range(k_count):
            terms = acc[s, k]
            real_part = terms[:pairs, :pairs] - terms[pairs:, pairs:]
            imaginary_part = terms[:pairs, pairs:] + terms[pairs:, :pairs]
            block = jnp.concatenate([real_part, imaginary_part], axis=1)

            @pl.when(flags[5] == k // own_k)
            def _():
                kept[above, k % own_k] = block

            @pl.when(flags[5] != k // own_k)
            def _():
                given[above, k % own_k] = block


def both_products(flags, chunks, of_end, of_mid, matched, sums):
    n_slots, k_count, both, _ = sums.shape
    depth = 4 * chunks[0][2][0].shape[0]
    columns = tuple((first, width) for first, width, _, _ in chunks)
    span = sum(width for _, width in columns)
    chosen = list(of_end) + list(of_mid) + list(matched)
    operands = [ref for _, _, blocks, _ in chunks for ref in blocks] + [ref for ref, _ in chosen] + [sums]
    halves = jax.ShapeDtypeStruct((n_slots, k_count // 2, both // 2, both), jnp.float32)
    return pl.pallas_call(
        functools.partial(
            both_kernel,
            n_slots=n_slots,
            columns=columns,
            places=tuple(places for _, _, _, places in chunks),
            leads=tuple(lead for _, lead in chosen),
        ),
        out_shape=(halves, halves),
        in_specs=[IN_SMEM] + [ANYWHERE] * len(operands),
        out_specs=(IN_VMEM, IN_VMEM),
        scratch_shapes=[
            pltpu.VMEM((2, depth, span), jnp.bfloat16),
            pltpu.VMEM((n_slots, k_count, both, depth), jnp.bfloat16),
            pltpu.VMEM((n_slots, k_count, both, span), jnp.bfloat16),
            pltpu.VMEM((k_count, both, span), jnp.float32),
            pltpu.VMEM((n_slots, k_count, both, both), jnp.float32),
            pltpu.SemaphoreType.DMA((span // STEP, 8)),
            pltpu.SemaphoreType.DMA((n_slots,)),
            pltpu.SemaphoreType.DMA((n_slots,)),
            pltpu.SemaphoreType.DMA,
        ],
        compiler_params=PARAMS,
        cost_estimate=COST,
        name="both_products",
    )(flags, *operands)


def turn_kernel(flags, first, second, first_turned, second_turned, turned_pair):
    first_turned[0] = first[0].T
    second_turned[0] = second[0].T
    turned_pair[0, 0] = second_turned[0]
    turned_pair[1, 0] = first_turned[0]


def turned_parts(flags, densities):
    k_count, n_rows, both = densities.shape
    quarter = n_rows // 4

    def part(which):
        return pl.BlockSpec((1, quarter, both), lambda k, flags: (k, flags[which], 0))

    one = pl.BlockSpec((1, both, quarter), lambda k, flags: (k, 0, 0))
    first, second, both_parts = pl.pallas_call(
        turn_kernel,
        out_shape=(
            jax.ShapeDtypeStruct((k_count, both, quarter), densities.dtype),
            jax.ShapeDtypeStruct((k_count, both, quarter), densities.dtype),
            jax.ShapeDtypeStruct((2, k_count, both, quarter), densities.dtype),
        ),
        grid_spec=pltpu.PrefetchScalarGridSpec(
            num_scalar_prefetch=1,
            grid=(k_count,),
            in_specs=[part(6), part(7)],
            out_specs=[
                one,
                one,
                pl.BlockSpec((2, 1, both, quarter), lambda k, flags: (0, k, 0, 0)),
            ],
        ),
        compiler_params=PARAMS,
        cost_estimate=COST,
        name="turned_parts",
    )(flags, densities, densities)
    return first, second, both_parts.reshape(2 * k_count, both, quarter)


def body(densities, screened, partner, pair_order):
    k_count, n_rows, both = densities.shape
    pair_count = both // 2
    quarter = n_rows // 4
    panel = screened.shape[2]
    widths = (panel // 2, panel // 4, panel // 4)
    firsts = [sum(widths[:n]) for n in range(3)]
    k_owner = lax.axis_index("ka")
    c = lax.axis_index("ga")
    z, b = k_owner // 4, k_owner % 4
    half, odd = z // 2, z % 2
    offset = partner[0] % k_count
    ends = (z == 0) | (z == 3)
    flags = jnp.stack([b, c == odd, half, offset, ends, c, 2 * (1 - odd) + c, 2 * odd + c]).astype(jnp.int32)
    rows = screened.shape[1]

    part = (k_count, both, quarter)

    def own_pieces(n, when, at=0):
        first, width = firsts[n], widths[n]
        return [
            (when, screened, real(first, width), columns_of(at, width)),
            (when, screened, imaginary(first, width), columns_of(at + width, width)),
        ]

    def far_part(*numbers):
        pieces, at = [], 0
        for n in numbers:
            pieces += own_pieces(n, own_far, at)
            at += 2 * widths[n]
        return (rows, at), pieces

    def sent_far(value):
        return moved(value, lambda z, b, c: (z ^ 1, b, 1 - c) if c != z % 2 else None)

    def panel_parts(n, arrived, at=0, before=None):
        copies = 0 if before is None else 1
        pieces = [piece + (copies,) for piece in own_pieces(n, own_near)]
        pieces.append((own_far, arrived, columns_of(at, 2 * widths[n]), columns_of(0, 2 * widths[n]), copies))
        if before is None:
            return (((rows, 2 * widths[n]), pieces),)
        x_side, y_side = before
        passed = widths[n - 1]
        shape, place = (rows, 2 * widths[n] + passed), columns_of(2 * widths[n], passed)
        return (
            (shape, pieces + [(always, y_side, columns_of(passed, passed), place)]),
            (shape, [(always, x_side, columns_of(0, passed), place)]),
        )

    first_part, second_part = slots_from(0, k_count), slots_from(k_count, k_count)

    flags, sent_0, sent_1 = moves(flags, (), far_part(0), far_part(1))
    arrived_0, arrived_1 = sent_far(sent_0), sent_far(sent_1)
    own_first, own_second, own_both = turned_parts(flags, densities)
    swapped_0 = other_core(own_second)
    pair_a, mid_ad = end_with_mid(own_first), mid_with_mid(own_both)

    flags, panel_0, sent_2 = moves(flags, (swapped_0,), *panel_parts(0, arrived_0), far_part(2))
    x_0, y_0 = along_x(panel_0), along_y(panel_0)

    flags, to_pair, to_mid = moves(
        flags,
        (),
        (part, [(at_end, own_second, whole, whole), (at_mid, mid_ad, first_part, whole)]),
        (part, [(always, pair_a, whole, whole)]),
    )
    pair_b, mid_b = end_with_mid(to_pair), mid_with_mid(to_mid)

    flags, to_x, to_y, sent_2 = moves(flags, (), *panel_parts(1, arrived_1, 0, (x_0, y_0)), passing=(sent_2,))
    x_1, y_1 = along_x(to_x), along_y(to_y)
    panel_1 = to_x
    arrived_2 = sent_far(sent_2)

    chunk_0 = (firsts[0], widths[0], (panel_0, x_0, y_0, y_0, x_0), (widths[0], 0, 0))
    early_end, early_mid = [(own_second, 0), (pair_a, 0)], [(own_first, 0), (mid_ad, 0)]
    left_0, flags = first_product(flags, [chunk_0], (0, 1, 2), 0, 2, early_end, early_mid)

    flags, pair_b, mid_b = moves(flags, (arrived_2,), passing=(pair_b, mid_b))
    swapped_a = other_core(pair_a)
    pair_c, mid_c = mid_to_end(mid_b), mid_with_mid(pair_b)
    of_end = [(own_second, 0), (pair_a, 0), (pair_b, 0), None]
    of_mid = [(own_first, 0), (mid_ad, 0), (mid_b, 0), (pair_b, 0)]
    every = (0, 1, 2, 3)

    flags, to_x, to_y = moves(flags, (), *panel_parts(2, arrived_2, 0, (x_1, y_1)))
    x_2, y_2 = along_x(to_x), along_y(to_y)
    panel_2 = to_x
    chunk_0 = (firsts[0], widths[0], (panel_0, x_0, y_0, y_1, x_1), (widths[0], 2 * widths[1], 2 * widths[1]))
    left_2, flags = first_product(flags, [chunk_0], every, 2, 1, of_end, of_mid)

    flags, late_1, late_2 = moves(
        flags,
        (swapped_a,),
        (part, [(at_end, pair_b, whole, whole), (at_mid, mid_ad, second_part, whole)]),
        (part, [(at_end, pair_c, whole, whole), (at_mid, mid_c, whole, whole)]),
    )
    swapped_1, swapped_2 = other_core(late_1), other_core(late_2)
    of_end[3] = (pair_c, 0)
    matched = [(own_second, 0), (swapped_0, 0), (pair_a, 0), (swapped_a, 0)]
    matched += [(late_1, 0), (swapped_1, 0), (late_2, 0), (swapped_2, 0)]
    left_3, flags = first_product(flags, [chunk_0], every, 3, 1, of_end, of_mid)

    shape = (rows, widths[2])
    flags, to_x, to_y = moves(
        flags,
        (),
        (shape, [(always, y_2, columns_of(widths[2], widths[2]), whole)]),
        (shape, [(always, x_2, columns_of(0, widths[2]), whole)]),
    )
    x_3, y_3 = along_x(to_x), along_y(to_y)
    chunk_1 = (firsts[1], widths[1], (panel_1, x_1, y_1, y_2, x_2), (widths[1], 2 * widths[2], 2 * widths[2]))
    sums_0, flags = stored_products(flags, chunk_0, of_end, of_mid, matched, [left_0, left_2, left_3])
    chunk_2 = (firsts[2], widths[2], (panel_2, x_2, y_2, y_3, x_3), (widths[2], 0, 0))
    mine, given = both_products(flags, [chunk_1, chunk_2], of_end, of_mid, matched, sums_0)

    mine = mine + other_core(given)
    total = jnp.stack([mine[0], mine[3]])
    for shift in (1, 2, 3):
        sent = jnp.stack([mine[shift], mine[shift - 1]])
        total = total + moved(sent, lambda z, b, c: ((z + shift) % 4, b, c))
    theirs = other_core(total)
    total = jnp.where(c == 0, jnp.concatenate([total, theirs], axis=1), jnp.concatenate([theirs, total], axis=1))
    total = total.reshape(2 * k_count, pair_count, both)
    order_table = (jnp.arange(pair_count)[:, None] == pair_order[None, :]).astype(jnp.float32)
    filed = reorder(total[:, :, :pair_count], total[:, :, pair_count:], order_table)
    sources = (jnp.arange(k_count) - offset) % k_count
    mirror = conjugate_side(jnp.take(filed[k_count:], sources, axis=0), pair_count)
    return (filed[:k_count], mirror)


def solution(mesh):
    in_specs = (P("ka", None, None), P(None, "ka", "ga"), P(), P())
    out_specs = (P("ka", None, None), P("ka", None, None))
    planes = mesh.shape["ka"] == 16 and mesh.shape["ga"] == 2
    chosen = body if planes else general_body
    return jax.shard_map(chosen, mesh=mesh, in_specs=in_specs, out_specs=out_specs, check_vma=False)
```

```python
import functools

import jax
import jax.numpy as jnp
from jax import lax
from jax.experimental import pallas as pl
from jax.experimental.pallas import tpu as pltpu
from jax.sharding import PartitionSpec as P


def passed_along(value, axis, steps):
    count = lax.axis_size(axis)
    pairs = [(source, (source + steps) % count) for source in range(count)]
    return lax.ppermute(value, axis, pairs)


def conjugate_side(blocks, pair_count):
    real_half = jnp.swapaxes(blocks[:, :, :pair_count], 1, 2)
    imag_half = jnp.swapaxes(blocks[:, :, pair_count:], 1, 2)
    return jnp.concatenate([real_half, -imag_half], axis=2)


def combine_terms(partial_value, order_table, pair_count):
    block_re = partial_value[:, 0, :, :pair_count] - partial_value[:, 1, :, pair_count:]
    block_im = partial_value[:, 0, :, pair_count:] + partial_value[:, 1, :, :pair_count]
    return reorder(block_re, block_im, order_table)


def reorder(block_re, block_im, order_table):
    block_re = jnp.einsum("kpq,qj->kpj", block_re, order_table, precision=lax.Precision.HIGHEST)
    block_im = jnp.einsum("kpq,qj->kpj", block_im, order_table, precision=lax.Precision.HIGHEST)
    return jnp.concatenate([block_re, block_im], axis=2)


def finish_terms(left_sums, matched, pair_count):
    left_re = left_sums[:, 0, :pair_count] + left_sums[:, 1, pair_count:]
    left_im = left_sums[:, 1, :pair_count] - left_sums[:, 0, pair_count:]
    left_factor = jnp.stack([left_re, left_im], axis=1)
    return jnp.einsum(
        "kwpc,kcq->kwpq", left_factor, matched.astype(jnp.float32), precision=lax.Precision.HIGHEST
    )


def general_body(densities, screened, partner, pair_order):
    k_count = densities.shape[0]
    pair_count = densities.shape[2] // 2
    panel_width = screened.shape[2]
    k_owner = lax.axis_index("ka")
    column = lax.axis_index("ga")
    own_columns = lax.dynamic_slice_in_dim(densities, column * panel_width, panel_width, 1)
    arrived = passed_along(own_columns, "ka", -4)
    own_partner = lax.dynamic_slice_in_dim(partner, k_owner * k_count, k_count, 0)
    slot_index = own_partner % k_count
    offset = slot_index[0]
    matched = jnp.take(arrived, slot_index, axis=0)
    left_sums = jnp.einsum(
        "kgp,wgc->kwpc",
        densities,
        lax.all_gather(screened, "ka", axis=1, tiled=True),
        preferred_element_type=jnp.float32,
    )
    partial_value = finish_terms(left_sums, matched, pair_count)
    order_table = (jnp.arange(pair_count)[:, None] == pair_order[None, :]).astype(jnp.float32)
    sources = (jnp.arange(k_count) - offset) % k_count
    summed = lax.psum(partial_value, "ga")
    direct = combine_terms(summed, order_table, pair_count)
    received = passed_along(direct, "ka", 4)
    mirror = conjugate_side(jnp.take(received, sources, axis=0), pair_count)
    return (direct, mirror)


AXES = ("ka", "ga")
STEP = 256
WIDE_STEP = 512


def device(z, b, c):
    return (z * 4 + b) * 2 + c


def moved(value, rule):
    pairs = []
    for z in range(4):
        for b in range(4):
            for c in range(2):
                target = rule(z, b, c)
                if target is not None:
                    pairs.append((device(z, b, c), device(*target)))
    return lax.ppermute(value, AXES, pairs)


def along_x(value):
    return moved(value, lambda z, b, c: (z, b ^ 1, c))


def along_y(value):
    return moved(value, lambda z, b, c: (z, b ^ 2, c))


def other_core(value):
    return moved(value, lambda z, b, c: (z, b, 1 - c))


def end_with_mid(value):
    return moved(value, lambda z, b, c: (z ^ 1, b, c))


def mid_to_end(value):
    return moved(value, lambda z, b, c: (z ^ 1, b, c) if z in (1, 2) else None)


def mid_with_mid(value):
    return moved(value, lambda z, b, c: (3 - z, b, c) if z in (1, 2) else None)


ANYWHERE = pl.BlockSpec(memory_space=pltpu.HBM)
IN_SMEM = pl.BlockSpec(memory_space=pltpu.SMEM)
IN_VMEM = pl.BlockSpec(memory_space=pltpu.VMEM)
PARAMS = pltpu.CompilerParams(vmem_limit_bytes=64 * 1024 * 1024)
COST = pl.CostEstimate(flops=1000, bytes_accessed=1000, transcendentals=0)
FLAGS = jax.ShapeDtypeStruct((8,), jnp.int32)


def keep_flags(flags, out):
    for i in range(flags.shape[0]):
        out[i] = flags[i]


def always(flags):
    return None


def at_end(flags):
    return flags[4] == 1


def at_mid(flags):
    return flags[4] == 0


def own_near(flags):
    return flags[1] == 1


def own_far(flags):
    return flags[1] == 0


def whole(ref):
    return ref


def real(first, width):
    return lambda ref: ref.at[0, :, first : first + width]


def imaginary(first, width):
    return lambda ref: ref.at[1, :, first : first + width]


def columns_of(first, width):
    return lambda ref: ref.at[:, first : first + width]


def slots_from(first, count):
    return lambda ref: ref.at[first : first + count]


def moves_kernel(flags, *refs, plan, n_sources, n_outs, n_passing):
    sources, outs = refs[:n_sources], refs[n_sources : n_sources + n_outs]
    flags_out, *stages = refs[n_sources + n_outs + n_passing : -2]
    in_sems, out_sems = refs[-2:]

    def run(chosen, act):
        if chosen is None:
            act()
        else:
            pl.when(chosen)(act)

    copies = []
    for i, (when, number, view, out_numbers, target) in enumerate(plan):
        stage = target(stages[out_numbers[0]])
        load = pltpu.make_async_copy(view(sources[number]), stage, in_sems.at[i])
        stores = [
            pltpu.make_async_copy(stage, target(outs[out_number]), out_sems.at[i, j])
            for j, out_number in enumerate(out_numbers)
        ]
        copies.append((when(flags), load, stores))
        run(when(flags), load.start)
    keep_flags(flags, flags_out)
    for chosen, load, stores in copies:
        def forward():
            load.wait()
            for store in stores:
                store.start()

        run(chosen, forward)
    for chosen, _, stores in copies:
        for store in stores:
            run(chosen, store.wait)


def moves(flags, waits, *outputs, passing=()):
    sources, plan = [], []
    for number, (_, pieces) in enumerate(outputs):
        for when, source, view, target, *more in pieces:
            plan.append((when, len(sources), view, tuple(range(number, number + 1 + sum(more))), target))
            sources.append(source)
    operands = sources + list(waits)
    shapes = [jax.ShapeDtypeStruct(shape, jnp.bfloat16) for shape, _ in outputs]
    aliases = {1 + len(operands) + i: len(outputs) + i for i in range(len(passing))}
    operands += list(passing)
    shapes += [jax.ShapeDtypeStruct(value.shape, value.dtype) for value in passing]
    results = pl.pallas_call(
        functools.partial(
            moves_kernel, plan=tuple(plan), n_sources=len(operands), n_outs=len(outputs), n_passing=len(passing)
        ),
        out_shape=tuple(shapes) + (FLAGS,),
        in_specs=[IN_SMEM] + [ANYWHERE] * len(operands),
        out_specs=(ANYWHERE,) * len(shapes) + (IN_SMEM,),
        input_output_aliases=aliases,
        scratch_shapes=[pltpu.VMEM(shape, jnp.bfloat16) for shape, _ in outputs]
        + [pltpu.SemaphoreType.DMA((max(len(plan), 1),)), pltpu.SemaphoreType.DMA((max(len(plan), 1), 2))],
        compiler_params=PARAMS,
        cost_estimate=COST,
        name="moves",
    )(flags, *operands)
    return results[-1], *results[:-1]


def w_copies(blocks, places, turns, w_buf, source_at, target_at, step, sems):
    width, real_at, imaginary_at = places
    rows = w_buf.shape[1] // len(turns)
    copies = []
    for i, turn in enumerate(turns):
        for part in range(2):
            source = blocks[turn] if turn < 3 else blocks[3 + part]
            first = (real_at, imaginary_at)[part] if turn == 3 else part * width
            target = w_buf.at[part, i * rows : (i + 1) * rows, target_at : target_at + step]
            source = source.at[:, first + source_at : first + source_at + step]
            copies.append(pltpu.make_async_copy(source, target, sems.at[len(copies)]))
    return copies


def m_copies(flags, turns, end_part, mid_part, target, sem):
    rows = target.shape[2] // len(turns)
    for i, turn in enumerate(turns):
        start = pl.multiple_of((flags[0] ^ turn) * rows, rows)
        window = pl.ds(start, rows)
        place = target.at[:, :, i * rows : (i + 1) * rows]
        either(at_end(flags), end_part.at[:, :, window], mid_part.at[:, :, window], place, sem)


def part_of(ref, lead, count):
    return ref.at[lead : lead + count]


def either(chosen, first, second, target, sem):
    a = pltpu.make_async_copy(first, target, sem)
    b = pltpu.make_async_copy(second, target, sem)
    pl.when(chosen)(a.start)
    pl.when(jnp.logical_not(chosen))(b.start)
    return a


def matched_copies(flags, matched, leads, c_buf, slots, first, width, sems, first_slot=0):
    k_count = c_buf.shape[1]
    pairs = [[part_of(matched[2 * i + j], leads[2 * i + j], k_count) for j in range(2)] for i in range(4)]
    quarter = matched[0].shape[2]
    for s in slots:
        for half, s_matched in ((0, (first_slot + s + 1) % 4), (1, (first_slot + s - 1) % 4)):
            for end, order in ((1, (0, 1, 2, 3)), (0, (0, 2, 3, 1))):
                for number in range(2):
                    low, high = max(first, number * quarter), min(first + width, (number + 1) * quarter)
                    if low >= high:
                        continue
                    for core in range(2):
                        source = pairs[order[s_matched]][0 if core == number else 1]
                        copy = pltpu.make_async_copy(
                            source.at[:, :, low - number * quarter : high - number * quarter],
                            c_buf.at[s, :, :, low - first : high - first],
                            sems.at[s],
                        )
                        pl.when((flags[2] == half) & (flags[4] == end) & (flags[5] == core))(copy.start)


def matched_wait(c_buf, s, sems):
    pltpu.make_async_copy(c_buf.at[s], c_buf.at[s], sems.at[s]).wait()


def left_tile(lhs, w_re, w_im, k_count, both):
    re_side = jnp.dot(lhs, w_re, preferred_element_type=jnp.float32).reshape(k_count, both, -1)
    im_side = jnp.dot(lhs, w_im, preferred_element_type=jnp.float32).reshape(k_count, both, -1)
    pairs = both // 2
    left_re = re_side[:, :pairs] + im_side[:, pairs:]
    left_im = im_side[:, :pairs] - re_side[:, pairs:]
    return jnp.concatenate([left_re, left_im], axis=1)


def times_matched(left, matched):
    high_part = left.astype(jnp.bfloat16)
    low_part = (left - high_part.astype(jnp.float32)).astype(jnp.bfloat16)
    rows = left.shape[0]
    both_parts = jnp.concatenate([high_part, low_part], axis=0)
    dims = (((1,), (1,)), ((), ()))
    added = lax.dot_general(both_parts, matched, dims, preferred_element_type=jnp.float32)
    return added[:rows] + added[rows:]


def first_kernel(flags, *refs, first_slot, n_slots, columns, places, leads, turns, step):
    n_chunks = len(columns)
    w_refs = [refs[5 * i : 5 * i + 5] for i in range(n_chunks)]
    rest = refs[5 * n_chunks :]
    of_end, of_mid = rest[:n_slots], rest[n_slots : 2 * n_slots]
    left, flags_out, w_buf, m_buf, out_buf, w_sems, m_sems, out_sems = rest[2 * n_slots :]
    depth = w_buf.shape[1]
    _, k_count, both, _ = m_buf.shape
    copies, used = [], 0
    for i in range(n_chunks):
        for at in range(0, columns[i][1], step):
            copies.append(w_copies(w_refs[i], places[i], turns, w_buf, at, used, step, w_sems.at[used // step]))
            used += step
    total = used // step
    for s in range(max(n_slots, len(copies))):
        if s < len(copies):
            for copy in copies[s]:
                copy.start()
        if s < n_slots:
            end_part, mid_part = part_of(of_end[s], leads[s], k_count), part_of(of_mid[s], leads[n_slots + s], k_count)
            m_copies(flags, turns, end_part, mid_part, m_buf.at[s], m_sems.at[s])
    keep_flags(flags, flags_out)

    def out_copy(t):
        start = pl.multiple_of(t * step, STEP)
        target = left.at[:, :, :, pl.ds(start, step)]
        return pltpu.make_async_copy(out_buf.at[t % 2], target, out_sems.at[t % 2])

    def one_step(t, carry):
        @pl.when(t >= 2)
        def _():
            out_copy(t - 2).wait()

        for copy in w_copies(w_refs[0], places[0], turns, w_buf, 0, 0, step, w_sems.at[t]):
            copy.wait()
        @pl.when(t == 0)
        def _():
            for s in range(n_slots):
                pltpu.make_async_copy(m_buf.at[s], m_buf.at[s], m_sems.at[s]).wait()

        for at in range(0, step, STEP):
            start = pl.multiple_of(t * step + at, STEP)
            for s in range(n_slots):
                lhs = m_buf[s].reshape(k_count * both, depth)
                w_re, w_im = w_buf[0, :, pl.ds(start, STEP)], w_buf[1, :, pl.ds(start, STEP)]
                out_buf[t % 2, s, :, :, at : at + STEP] = left_tile(lhs, w_re, w_im, k_count, both)
        out_copy(t).start()
        return carry

    lax.fori_loop(0, total, one_step, 0)
    for t in range(max(total - 2, 0), total):
        out_copy(t).wait()


def first_product(flags, chunks, turns, first_slot, n_slots, of_end, of_mid):
    depth = len(turns) * chunks[0][2][0].shape[0]
    both, k_count = of_end[first_slot][0].shape[1], 4
    columns = tuple((first, width) for first, width, _, _ in chunks)
    span = sum(width for _, width in columns)
    slots = range(first_slot, first_slot + n_slots)
    step = WIDE_STEP if n_slots == 1 and all(width % WIDE_STEP == 0 for _, width in columns) else STEP
    chosen = [of_end[s] for s in slots] + [of_mid[s] for s in slots]
    operands = [ref for _, _, blocks, _ in chunks for ref in blocks] + [ref for ref, _ in chosen]
    return pl.pallas_call(
        functools.partial(
            first_kernel,
            first_slot=first_slot,
            n_slots=n_slots,
            columns=columns,
            places=tuple(places for _, _, _, places in chunks),
            leads=tuple(lead for _, lead in chosen),
            turns=turns,
            step=step,
        ),
        out_shape=(jax.ShapeDtypeStruct((n_slots, k_count, both, span), jnp.float32), FLAGS),
        in_specs=[IN_SMEM] + [ANYWHERE] * len(operands),
        out_specs=(ANYWHERE, IN_SMEM),
        scratch_shapes=[
            pltpu.VMEM((2, depth, span), jnp.bfloat16),
            pltpu.VMEM((n_slots, k_count, both, depth), jnp.bfloat16),
            pltpu.VMEM((2, n_slots, k_count, both, step), jnp.float32),
            pltpu.SemaphoreType.DMA((span // step, 8)),
            pltpu.SemaphoreType.DMA((n_slots,)),
            pltpu.SemaphoreType.DMA((2,)),
        ],
        compiler_params=PARAMS,
        cost_estimate=COST,
        name="first_product",
    )(flags, *operands)


def stored_kernel(flags, *refs, n_slots, n_lefts, columns, places, leads):
    first, width = columns
    w_refs, of_end, of_mid = refs[:5], refs[5 : 5 + n_slots], refs[5 + n_slots : 5 + 2 * n_slots]
    matched, rest = refs[5 + 2 * n_slots : 13 + 2 * n_slots], refs[13 + 2 * n_slots :]
    lefts, (sums, flags_out, w_buf, m_buf, c_buf, left_buf, w_sems, m_sems, c_sems, left_sems) = rest[:n_lefts], rest[n_lefts:]
    depth = w_buf.shape[1]
    all_slots, k_count, both, _ = c_buf.shape
    sources = [left.at[i] for left in lefts for i in range(left.shape[0])]
    w_loads = w_copies(w_refs, places, (3,), w_buf, 0, 0, width, w_sems)
    for copy in w_loads:
        copy.start()
    for s in range(all_slots):
        if s < n_slots:
            end_part, mid_part = part_of(of_end[s], leads[s], k_count), part_of(of_mid[s], leads[n_slots + s], k_count)
            m_copies(flags, (3,), end_part, mid_part, m_buf.at[s], m_sems.at[s])
        pltpu.make_async_copy(sources[s], left_buf.at[s], left_sems.at[s]).start()
        matched_copies(flags, matched, leads[2 * n_slots :], c_buf, (s,), first, width, c_sems)
    keep_flags(flags, flags_out)
    for copy in w_loads:
        copy.wait()

    def second(s):
        matched_wait(c_buf, s, c_sems)
        for k in range(k_count):
            sums[s, k] = times_matched(left_buf[s, k], c_buf[s, (k + flags[3]) % k_count])

    wide = WIDE_STEP if width % WIDE_STEP == 0 else STEP
    n_steps = width // wide

    def one_step(t, carry):
        s, step = t // n_steps, t % n_steps

        @pl.when(step == 0)
        def _():
            pltpu.make_async_copy(m_buf.at[s], m_buf.at[s], m_sems.at[s]).wait()
            pltpu.make_async_copy(left_buf.at[s], left_buf.at[s], left_sems.at[s]).wait()

        lhs = m_buf[s].reshape(k_count * both, depth)
        for at in range(0, wide, STEP):
            start = pl.multiple_of(step * wide + at, STEP)
            tile = left_tile(lhs, w_buf[0, :, pl.ds(start, STEP)], w_buf[1, :, pl.ds(start, STEP)], k_count, both)
            left_buf[s, :, :, pl.ds(start, STEP)] = left_buf[s, :, :, pl.ds(start, STEP)] + tile

        @pl.when(step == n_steps - 1)
        def _():
            second(s)

        return carry

    lax.fori_loop(0, n_slots * n_steps, one_step, 0)

    def only_second(s, carry):
        pltpu.make_async_copy(left_buf.at[s], left_buf.at[s], left_sems.at[s]).wait()
        second(s)
        return carry

    lax.fori_loop(n_slots, all_slots, only_second, 0)


def stored_products(flags, chunk, of_end, of_mid, matched, lefts):
    n_slots, k_count, both, _ = lefts[0].shape
    all_slots = sum(left.shape[0] for left in lefts)
    first, width, blocks, places = chunk
    rows = blocks[0].shape[0]
    chosen = list(of_end[:n_slots]) + list(of_mid[:n_slots]) + list(matched)
    operands = list(blocks) + [ref for ref, _ in chosen] + list(lefts)
    return pl.pallas_call(
        functools.partial(
            stored_kernel,
            n_slots=n_slots,
            n_lefts=len(lefts),
            columns=(first, width),
            places=places,
            leads=tuple(lead for _, lead in chosen),
        ),
        out_shape=(jax.ShapeDtypeStruct((all_slots, k_count, both, both), jnp.float32), FLAGS),
        in_specs=[IN_SMEM] + [ANYWHERE] * len(operands),
        out_specs=(IN_VMEM, IN_SMEM),
        scratch_shapes=[
            pltpu.VMEM((2, rows, width), jnp.bfloat16),
            pltpu.VMEM((n_slots, k_count, both, rows), jnp.bfloat16),
            pltpu.VMEM((all_slots, k_count, both, width), jnp.bfloat16),
            pltpu.VMEM((all_slots, k_count, both, width), jnp.float32),
            pltpu.SemaphoreType.DMA((2,)),
            pltpu.SemaphoreType.DMA((n_slots,)),
            pltpu.SemaphoreType.DMA((all_slots,)),
            pltpu.SemaphoreType.DMA((all_slots,)),
        ],
        compiler_params=PARAMS,
        cost_estimate=COST,
        name="stored_products",
    )(flags, *operands)


def both_kernel(flags, *refs, n_slots, columns, places, leads):
    n_chunks = len(columns)
    first = columns[0][0]
    w_refs, rest = [refs[5 * i : 5 * i + 5] for i in range(n_chunks)], refs[5 * n_chunks :]
    of_end, of_mid, rest = rest[:n_slots], rest[n_slots : 2 * n_slots], rest[2 * n_slots :]
    matched, sums_in, kept, given = rest[:8], rest[8], rest[9], rest[10]
    w_buf, m_buf, c_buf, left_buf, acc, w_sems, m_sems, c_sems, sums_sem = rest[11:]
    depth, span = w_buf.shape[1:]
    _, k_count, both, _ = m_buf.shape
    n_tiles = span // STEP
    turns = (0, 1, 2, 3)

    tiles = [(i, at) for i in range(n_chunks) for at in range(0, columns[i][1], STEP)]

    def w_tile(number):
        i, at = tiles[number]
        return w_copies(w_refs[i], places[i], turns, w_buf, at, number * STEP, STEP, w_sems.at[number])

    def m_start(s):
        end_part, mid_part = part_of(of_end[s], leads[s], k_count), part_of(of_mid[s], leads[n_slots + s], k_count)
        m_copies(flags, turns, end_part, mid_part, m_buf.at[s], m_sems.at[s])

    def c_start(s):
        matched_copies(flags, matched, leads[2 * n_slots :], c_buf, (s,), first, span, c_sems)

    for copy in w_tile(0):
        copy.start()
    m_start(0)
    for i in range(1, n_tiles):
        for copy in w_tile(i):
            copy.start()
    m_start(1)
    c_start(0)
    sums_copy = pltpu.make_async_copy(sums_in, acc, sums_sem)
    sums_copy.start()

    wide = WIDE_STEP if span % WIDE_STEP == 0 else STEP
    n_steps = span // wide

    def one_step(t, carry):
        s, step = t // n_steps, t % n_steps

        @pl.when(s == 0)
        def _():
            for i in range(wide // STEP):
                number = step * (wide // STEP) + i
                for copy in w_copies(w_refs[0], places[0], turns, w_buf, 0, 0, STEP, w_sems.at[number]):
                    copy.wait()

        @pl.when(step == 0)
        def _():
            pltpu.make_async_copy(m_buf.at[s], m_buf.at[s], m_sems.at[s]).wait()
            for j in range(n_slots - 1):
                @pl.when(s == j)
                def _():
                    if j + 2 < n_slots:
                        m_start(j + 2)
                    c_start(j + 1)

        lhs = m_buf[s].reshape(k_count * both, depth)
        for at in range(0, wide, STEP):
            start = pl.multiple_of(step * wide + at, STEP)
            tile = left_tile(lhs, w_buf[0, :, pl.ds(start, STEP)], w_buf[1, :, pl.ds(start, STEP)], k_count, both)
            left_buf[:, :, pl.ds(start, STEP)] = tile

        @pl.when(step == n_steps - 1)
        def _():
            @pl.when(s == 0)
            def _():
                sums_copy.wait()

            matched_wait(c_buf, s, c_sems)
            for k in range(k_count):
                acc[s, k] = acc[s, k] + times_matched(left_buf[k], c_buf[s, (k + flags[3]) % k_count])

        return carry

    lax.fori_loop(0, n_slots * n_steps, one_step, 0)
    pairs, own_k = both // 2, k_count // 2
    for s in range(n_slots):
        above = jnp.where(flags[2] == 0, s, (n_slots - s) % n_slots)
        for k in range(k_count):
            terms = acc[s, k]
            real_part = terms[:pairs, :pairs] - terms[pairs:, pairs:]
            imaginary_part = terms[:pairs, pairs:] + terms[pairs:, :pairs]
            block = jnp.concatenate([real_part, imaginary_part], axis=1)

            @pl.when(flags[5] == k // own_k)
            def _():
                kept[above, k % own_k] = block

            @pl.when(flags[5] != k // own_k)
            def _():
                given[above, k % own_k] = block


def both_products(flags, chunks, of_end, of_mid, matched, sums):
    n_slots, k_count, both, _ = sums.shape
    depth = 4 * chunks[0][2][0].shape[0]
    columns = tuple((first, width) for first, width, _, _ in chunks)
    span = sum(width for _, width in columns)
    chosen = list(of_end) + list(of_mid) + list(matched)
    operands = [ref for _, _, blocks, _ in chunks for ref in blocks] + [ref for ref, _ in chosen] + [sums]
    halves = jax.ShapeDtypeStruct((n_slots, k_count // 2, both // 2, both), jnp.float32)
    return pl.pallas_call(
        functools.partial(
            both_kernel,
            n_slots=n_slots,
            columns=columns,
            places=tuple(places for _, _, _, places in chunks),
            leads=tuple(lead for _, lead in chosen),
        ),
        out_shape=(halves, halves),
        in_specs=[IN_SMEM] + [ANYWHERE] * len(operands),
        out_specs=(IN_VMEM, IN_VMEM),
        scratch_shapes=[
            pltpu.VMEM((2, depth, span), jnp.bfloat16),
            pltpu.VMEM((n_slots, k_count, both, depth), jnp.bfloat16),
            pltpu.VMEM((n_slots, k_count, both, span), jnp.bfloat16),
            pltpu.VMEM((k_count, both, span), jnp.float32),
            pltpu.VMEM((n_slots, k_count, both, both), jnp.float32),
            pltpu.SemaphoreType.DMA((span // STEP, 8)),
            pltpu.SemaphoreType.DMA((n_slots,)),
            pltpu.SemaphoreType.DMA((n_slots,)),
            pltpu.SemaphoreType.DMA,
        ],
        compiler_params=PARAMS,
        cost_estimate=COST,
        name="both_products",
    )(flags, *operands)


def turn_kernel(flags, first, second, first_turned, second_turned, turned_pair):
    first_turned[0] = first[0].T
    second_turned[0] = second[0].T
    turned_pair[0, 0] = second_turned[0]
    turned_pair[1, 0] = first_turned[0]


def turned_parts(flags, densities):
    k_count, n_rows, both = densities.shape
    quarter = n_rows // 4

    def part(which):
        return pl.BlockSpec((1, quarter, both), lambda k, flags: (k, flags[which], 0))

    one = pl.BlockSpec((1, both, quarter), lambda k, flags: (k, 0, 0))
    first, second, both_parts = pl.pallas_call(
        turn_kernel,
        out_shape=(
            jax.ShapeDtypeStruct((k_count, both, quarter), densities.dtype),
            jax.ShapeDtypeStruct((k_count, both, quarter), densities.dtype),
            jax.ShapeDtypeStruct((2, k_count, both, quarter), densities.dtype),
        ),
        grid_spec=pltpu.PrefetchScalarGridSpec(
            num_scalar_prefetch=1,
            grid=(k_count,),
            in_specs=[part(6), part(7)],
            out_specs=[
                one,
                one,
                pl.BlockSpec((2, 1, both, quarter), lambda k, flags: (0, k, 0, 0)),
            ],
        ),
        compiler_params=PARAMS,
        cost_estimate=COST,
        name="turned_parts",
    )(flags, densities, densities)
    return first, second, both_parts.reshape(2 * k_count, both, quarter)


def body(densities, screened, partner, pair_order):
    k_count, n_rows, both = densities.shape
    pair_count = both // 2
    quarter = n_rows // 4
    panel = screened.shape[2]
    widths = (panel // 2, panel // 4, panel // 4)
    firsts = [sum(widths[:n]) for n in range(3)]
    k_owner = lax.axis_index("ka")
    c = lax.axis_index("ga")
    z, b = k_owner // 4, k_owner % 4
    half, odd = z // 2, z % 2
    offset = partner[0] % k_count
    ends = (z == 0) | (z == 3)
    flags = jnp.stack([b, c == odd, half, offset, ends, c, 2 * (1 - odd) + c, 2 * odd + c]).astype(jnp.int32)
    rows = screened.shape[1]

    part = (k_count, both, quarter)

    def own_pieces(n, when, at=0):
        first, width = firsts[n], widths[n]
        return [
            (when, screened, real(first, width), columns_of(at, width)),
            (when, screened, imaginary(first, width), columns_of(at + width, width)),
        ]

    def far_part(*numbers):
        pieces, at = [], 0
        for n in numbers:
            pieces += own_pieces(n, own_far, at)
            at += 2 * widths[n]
        return (rows, at), pieces

    def sent_far(value):
        return moved(value, lambda z, b, c: (z ^ 1, b, 1 - c) if c != z % 2 else None)

    def panel_parts(n, arrived, at=0, before=None):
        copies = 0 if before is None else 1
        pieces = [piece + (copies,) for piece in own_pieces(n, own_near)]
        pieces.append((own_far, arrived, columns_of(at, 2 * widths[n]), columns_of(0, 2 * widths[n]), copies))
        if before is None:
            return (((rows, 2 * widths[n]), pieces),)
        x_side, y_side = before
        passed = widths[n - 1]
        shape, place = (rows, 2 * widths[n] + passed), columns_of(2 * widths[n], passed)
        return (
            (shape, pieces + [(always, y_side, columns_of(passed, passed), place)]),
            (shape, [(always, x_side, columns_of(0, passed), place)]),
        )

    first_part, second_part = slots_from(0, k_count), slots_from(k_count, k_count)

    flags, sent_0 = moves(flags, (), far_part(0))
    arrived_0 = sent_far(sent_0)
    own_first, own_second, own_both = turned_parts(flags, densities)
    swapped_0 = other_core(own_second)
    pair_a, mid_ad = end_with_mid(own_first), mid_with_mid(own_both)

    flags, sent_1, sent_2 = moves(flags, (own_first,), far_part(1), far_part(2))

    flags, panel_0 = moves(flags, (swapped_0,), *panel_parts(0, arrived_0))
    arrived_1 = sent_far(sent_1)
    x_0, y_0 = along_x(panel_0), along_y(panel_0)

    flags, to_pair, to_mid = moves(
        flags,
        (),
        (part, [(at_end, own_second, whole, whole), (at_mid, mid_ad, first_part, whole)]),
        (part, [(always, pair_a, whole, whole)]),
    )
    pair_b, mid_b = end_with_mid(to_pair), mid_with_mid(to_mid)

    flags, to_x, to_y, sent_2 = moves(flags, (), *panel_parts(1, arrived_1, 0, (x_0, y_0)), passing=(sent_2,))
    x_1, y_1 = along_x(to_x), along_y(to_y)
    panel_1 = to_x
    arrived_2 = sent_far(sent_2)

    chunk_0 = (firsts[0], widths[0], (panel_0, x_0, y_0, y_0, x_0), (widths[0], 0, 0))
    early_end, early_mid = [(own_second, 0), (pair_a, 0)], [(own_first, 0), (mid_ad, 0)]
    left_0, flags = first_product(flags, [chunk_0], (0, 1, 2), 0, 2, early_end, early_mid)

    flags, pair_b, mid_b = moves(flags, (arrived_2,), passing=(pair_b, mid_b))
    swapped_a = other_core(pair_a)
    pair_c, mid_c = mid_to_end(mid_b), mid_with_mid(pair_b)
    of_end = [(own_second, 0), (pair_a, 0), (pair_b, 0), None]
    of_mid = [(own_first, 0), (mid_ad, 0), (mid_b, 0), (pair_b, 0)]
    every = (0, 1, 2, 3)

    flags, to_x, to_y = moves(flags, (), *panel_parts(2, arrived_2, 0, (x_1, y_1)))
    x_2, y_2 = along_x(to_x), along_y(to_y)
    panel_2 = to_x
    chunk_0 = (firsts[0], widths[0], (panel_0, x_0, y_0, y_1, x_1), (widths[0], 2 * widths[1], 2 * widths[1]))
    left_2, flags = first_product(flags, [chunk_0], every, 2, 1, of_end, of_mid)

    flags, late_1, late_2 = moves(
        flags,
        (swapped_a,),
        (part, [(at_end, pair_b, whole, whole), (at_mid, mid_ad, second_part, whole)]),
        (part, [(at_end, pair_c, whole, whole), (at_mid, mid_c, whole, whole)]),
    )
    swapped_1, swapped_2 = other_core(late_1), other_core(late_2)
    of_end[3] = (pair_c, 0)
    matched = [(own_second, 0), (swapped_0, 0), (pair_a, 0), (swapped_a, 0)]
    matched += [(late_1, 0), (swapped_1, 0), (late_2, 0), (swapped_2, 0)]
    left_3, flags = first_product(flags, [chunk_0], every, 3, 1, of_end, of_mid)

    shape = (rows, widths[2])
    flags, to_x, to_y = moves(
        flags,
        (),
        (shape, [(always, y_2, columns_of(widths[2], widths[2]), whole)]),
        (shape, [(always, x_2, columns_of(0, widths[2]), whole)]),
    )
    x_3, y_3 = along_x(to_x), along_y(to_y)
    chunk_1 = (firsts[1], widths[1], (panel_1, x_1, y_1, y_2, x_2), (widths[1], 2 * widths[2], 2 * widths[2]))
    sums_0, flags = stored_products(flags, chunk_0, of_end, of_mid, matched, [left_0, left_2, left_3])
    chunk_2 = (firsts[2], widths[2], (panel_2, x_2, y_2, y_3, x_3), (widths[2], 0, 0))
    mine, given = both_products(flags, [chunk_1, chunk_2], of_end, of_mid, matched, sums_0)

    mine = mine + other_core(given)
    total = jnp.stack([mine[0], mine[3]])
    for shift in (1, 2, 3):
        sent = jnp.stack([mine[shift], mine[shift - 1]])
        total = total + moved(sent, lambda z, b, c: ((z + shift) % 4, b, c))
    theirs = other_core(total)
    total = jnp.where(c == 0, jnp.concatenate([total, theirs], axis=1), jnp.concatenate([theirs, total], axis=1))
    total = total.reshape(2 * k_count, pair_count, both)
    order_table = (jnp.arange(pair_count)[:, None] == pair_order[None, :]).astype(jnp.float32)
    filed = reorder(total[:, :, :pair_count], total[:, :, pair_count:], order_table)
    sources = (jnp.arange(k_count) - offset) % k_count
    mirror = conjugate_side(jnp.take(filed[k_count:], sources, axis=0), pair_count)
    return (filed[:k_count], mirror)


def solution(mesh):
    in_specs = (P("ka", None, None), P(None, "ka", "ga"), P(), P())
    out_specs = (P("ka", None, None), P("ka", None, None))
    planes = mesh.shape["ka"] == 16 and mesh.shape["ga"] == 2
    chosen = body if planes else general_body
    return jax.shard_map(chosen, mesh=mesh, in_specs=in_specs, out_specs=out_specs, check_vma=False)
```

```python
import functools

import jax
import jax.numpy as jnp
from jax import lax
from jax.experimental import pallas as pl
from jax.experimental.pallas import tpu as pltpu
from jax.sharding import PartitionSpec as P


def passed_along(value, axis, steps):
    count = lax.axis_size(axis)
    pairs = [(source, (source + steps) % count) for source in range(count)]
    return lax.ppermute(value, axis, pairs)


def conjugate_side(blocks, pair_count):
    real_half = jnp.swapaxes(blocks[:, :, :pair_count], 1, 2)
    imag_half = jnp.swapaxes(blocks[:, :, pair_count:], 1, 2)
    return jnp.concatenate([real_half, -imag_half], axis=2)


def combine_terms(partial_value, order_table, pair_count):
    block_re = partial_value[:, 0, :, :pair_count] - partial_value[:, 1, :, pair_count:]
    block_im = partial_value[:, 0, :, pair_count:] + partial_value[:, 1, :, :pair_count]
    return reorder(block_re, block_im, order_table)


def reorder(block_re, block_im, order_table):
    block_re = jnp.einsum("kpq,qj->kpj", block_re, order_table, precision=lax.Precision.HIGHEST)
    block_im = jnp.einsum("kpq,qj->kpj", block_im, order_table, precision=lax.Precision.HIGHEST)
    return jnp.concatenate([block_re, block_im], axis=2)


def finish_terms(left_sums, matched, pair_count):
    left_re = left_sums[:, 0, :pair_count] + left_sums[:, 1, pair_count:]
    left_im = left_sums[:, 1, :pair_count] - left_sums[:, 0, pair_count:]
    left_factor = jnp.stack([left_re, left_im], axis=1)
    return jnp.einsum(
        "kwpc,kcq->kwpq", left_factor, matched.astype(jnp.float32), precision=lax.Precision.HIGHEST
    )


def general_body(densities, screened, partner, pair_order):
    k_count = densities.shape[0]
    pair_count = densities.shape[2] // 2
    panel_width = screened.shape[2]
    k_owner = lax.axis_index("ka")
    column = lax.axis_index("ga")
    own_columns = lax.dynamic_slice_in_dim(densities, column * panel_width, panel_width, 1)
    arrived = passed_along(own_columns, "ka", -4)
    own_partner = lax.dynamic_slice_in_dim(partner, k_owner * k_count, k_count, 0)
    slot_index = own_partner % k_count
    offset = slot_index[0]
    matched = jnp.take(arrived, slot_index, axis=0)
    left_sums = jnp.einsum(
        "kgp,wgc->kwpc",
        densities,
        lax.all_gather(screened, "ka", axis=1, tiled=True),
        preferred_element_type=jnp.float32,
    )
    partial_value = finish_terms(left_sums, matched, pair_count)
    order_table = (jnp.arange(pair_count)[:, None] == pair_order[None, :]).astype(jnp.float32)
    sources = (jnp.arange(k_count) - offset) % k_count
    summed = lax.psum(partial_value, "ga")
    direct = combine_terms(summed, order_table, pair_count)
    received = passed_along(direct, "ka", 4)
    mirror = conjugate_side(jnp.take(received, sources, axis=0), pair_count)
    return (direct, mirror)


AXES = ("ka", "ga")
STEP = 256
WIDE_STEP = 512


def device(z, b, c):
    return (z * 4 + b) * 2 + c


def moved(value, rule):
    pairs = []
    for z in range(4):
        for b in range(4):
            for c in range(2):
                target = rule(z, b, c)
                if target is not None:
                    pairs.append((device(z, b, c), device(*target)))
    return lax.ppermute(value, AXES, pairs)


def along_x(value):
    return moved(value, lambda z, b, c: (z, b ^ 1, c))


def along_y(value):
    return moved(value, lambda z, b, c: (z, b ^ 2, c))


def other_core(value):
    return moved(value, lambda z, b, c: (z, b, 1 - c))


def end_with_mid(value):
    return moved(value, lambda z, b, c: (z ^ 1, b, c))


def mid_to_end(value):
    return moved(value, lambda z, b, c: (z ^ 1, b, c) if z in (1, 2) else None)


def mid_with_mid(value):
    return moved(value, lambda z, b, c: (3 - z, b, c) if z in (1, 2) else None)


ANYWHERE = pl.BlockSpec(memory_space=pltpu.HBM)
IN_SMEM = pl.BlockSpec(memory_space=pltpu.SMEM)
IN_VMEM = pl.BlockSpec(memory_space=pltpu.VMEM)
PARAMS = pltpu.CompilerParams(vmem_limit_bytes=64 * 1024 * 1024)
COST = pl.CostEstimate(flops=1000, bytes_accessed=1000, transcendentals=0)
FLAGS = jax.ShapeDtypeStruct((8,), jnp.int32)


def keep_flags(flags, out):
    for i in range(flags.shape[0]):
        out[i] = flags[i]


def always(flags):
    return None


def at_end(flags):
    return flags[4] == 1


def at_mid(flags):
    return flags[4] == 0


def own_near(flags):
    return flags[1] == 1


def own_far(flags):
    return flags[1] == 0


def whole(ref):
    return ref


def real(first, width):
    return lambda ref: ref.at[0, :, first : first + width]


def imaginary(first, width):
    return lambda ref: ref.at[1, :, first : first + width]


def columns_of(first, width):
    return lambda ref: ref.at[:, first : first + width]


def slots_from(first, count):
    return lambda ref: ref.at[first : first + count]


def moves_kernel(flags, *refs, plan, n_sources, n_outs, n_passing):
    sources, outs = refs[:n_sources], refs[n_sources : n_sources + n_outs]
    flags_out, *stages = refs[n_sources + n_outs + n_passing : -2]
    in_sems, out_sems = refs[-2:]

    def run(chosen, act):
        if chosen is None:
            act()
        else:
            pl.when(chosen)(act)

    copies = []
    for i, (when, number, view, out_numbers, target) in enumerate(plan):
        stage = target(stages[out_numbers[0]])
        load = pltpu.make_async_copy(view(sources[number]), stage, in_sems.at[i])
        stores = [
            pltpu.make_async_copy(stage, target(outs[out_number]), out_sems.at[i, j])
            for j, out_number in enumerate(out_numbers)
        ]
        copies.append((when(flags), load, stores))
        run(when(flags), load.start)
    keep_flags(flags, flags_out)
    for chosen, load, stores in copies:
        def forward():
            load.wait()
            for store in stores:
                store.start()

        run(chosen, forward)
    for chosen, _, stores in copies:
        for store in stores:
            run(chosen, store.wait)


def moves(flags, waits, *outputs, passing=()):
    sources, plan = [], []
    for number, (_, pieces) in enumerate(outputs):
        for when, source, view, target, *more in pieces:
            plan.append((when, len(sources), view, tuple(range(number, number + 1 + sum(more))), target))
            sources.append(source)
    operands = sources + list(waits)
    shapes = [jax.ShapeDtypeStruct(shape, jnp.bfloat16) for shape, _ in outputs]
    aliases = {1 + len(operands) + i: len(outputs) + i for i in range(len(passing))}
    operands += list(passing)
    shapes += [jax.ShapeDtypeStruct(value.shape, value.dtype) for value in passing]
    results = pl.pallas_call(
        functools.partial(
            moves_kernel, plan=tuple(plan), n_sources=len(operands), n_outs=len(outputs), n_passing=len(passing)
        ),
        out_shape=tuple(shapes) + (FLAGS,),
        in_specs=[IN_SMEM] + [ANYWHERE] * len(operands),
        out_specs=(ANYWHERE,) * len(shapes) + (IN_SMEM,),
        input_output_aliases=aliases,
        scratch_shapes=[pltpu.VMEM(shape, jnp.bfloat16) for shape, _ in outputs]
        + [pltpu.SemaphoreType.DMA((max(len(plan), 1),)), pltpu.SemaphoreType.DMA((max(len(plan), 1), 2))],
        compiler_params=PARAMS,
        cost_estimate=COST,
        name="moves",
    )(flags, *operands)
    return results[-1], *results[:-1]


def w_copies(blocks, places, turns, w_buf, source_at, target_at, step, sems):
    width, real_at, imaginary_at = places
    rows = w_buf.shape[1] // len(turns)
    copies = []
    for i, turn in enumerate(turns):
        for part in range(2):
            source = blocks[turn] if turn < 3 else blocks[3 + part]
            first = (real_at, imaginary_at)[part] if turn == 3 else part * width
            target = w_buf.at[part, i * rows : (i + 1) * rows, target_at : target_at + step]
            source = source.at[:, first + source_at : first + source_at + step]
            copies.append(pltpu.make_async_copy(source, target, sems.at[len(copies)]))
    return copies


def m_copies(flags, turns, end_part, mid_part, target, sem):
    rows = target.shape[2] // len(turns)
    for i, turn in enumerate(turns):
        start = pl.multiple_of((flags[0] ^ turn) * rows, rows)
        window = pl.ds(start, rows)
        place = target.at[:, :, i * rows : (i + 1) * rows]
        either(at_end(flags), end_part.at[:, :, window], mid_part.at[:, :, window], place, sem)


def part_of(ref, lead, count):
    return ref.at[lead : lead + count]


def either(chosen, first, second, target, sem):
    a = pltpu.make_async_copy(first, target, sem)
    b = pltpu.make_async_copy(second, target, sem)
    pl.when(chosen)(a.start)
    pl.when(jnp.logical_not(chosen))(b.start)
    return a


def matched_copies(flags, matched, leads, c_buf, slots, first, width, sems, first_slot=0):
    k_count = c_buf.shape[1]
    pairs = [[part_of(matched[2 * i + j], leads[2 * i + j], k_count) for j in range(2)] for i in range(4)]
    quarter = matched[0].shape[2]
    for s in slots:
        for half, s_matched in ((0, (first_slot + s + 1) % 4), (1, (first_slot + s - 1) % 4)):
            for end, order in ((1, (0, 1, 2, 3)), (0, (0, 2, 3, 1))):
                for number in range(2):
                    low, high = max(first, number * quarter), min(first + width, (number + 1) * quarter)
                    if low >= high:
                        continue
                    for core in range(2):
                        source = pairs[order[s_matched]][0 if core == number else 1]
                        copy = pltpu.make_async_copy(
                            source.at[:, :, low - number * quarter : high - number * quarter],
                            c_buf.at[s, :, :, low - first : high - first],
                            sems.at[s],
                        )
                        pl.when((flags[2] == half) & (flags[4] == end) & (flags[5] == core))(copy.start)


def matched_wait(c_buf, s, sems):
    pltpu.make_async_copy(c_buf.at[s], c_buf.at[s], sems.at[s]).wait()


def left_tile(lhs, w_re, w_im, k_count, both):
    re_side = jnp.dot(lhs, w_re, preferred_element_type=jnp.float32).reshape(k_count, both, -1)
    im_side = jnp.dot(lhs, w_im, preferred_element_type=jnp.float32).reshape(k_count, both, -1)
    pairs = both // 2
    left_re = re_side[:, :pairs] + im_side[:, pairs:]
    left_im = im_side[:, :pairs] - re_side[:, pairs:]
    return jnp.concatenate([left_re, left_im], axis=1)


def times_matched(left, matched):
    high_part = left.astype(jnp.bfloat16)
    low_part = (left - high_part.astype(jnp.float32)).astype(jnp.bfloat16)
    rows = left.shape[0]
    both_parts = jnp.concatenate([high_part, low_part], axis=0)
    dims = (((1,), (1,)), ((), ()))
    added = lax.dot_general(both_parts, matched, dims, preferred_element_type=jnp.float32)
    return added[:rows] + added[rows:]


def first_kernel(flags, *refs, first_slot, n_slots, columns, places, leads, turns, step):
    n_chunks = len(columns)
    w_refs = [refs[5 * i : 5 * i + 5] for i in range(n_chunks)]
    rest = refs[5 * n_chunks :]
    of_end, of_mid = rest[:n_slots], rest[n_slots : 2 * n_slots]
    left, flags_out, w_buf, m_buf, out_buf, w_sems, m_sems, out_sems = rest[2 * n_slots :]
    depth = w_buf.shape[1]
    _, k_count, both, _ = m_buf.shape
    copies, used = [], 0
    for i in range(n_chunks):
        for at in range(0, columns[i][1], step):
            copies.append(w_copies(w_refs[i], places[i], turns, w_buf, at, used, step, w_sems.at[used // step]))
            used += step
    total = used // step
    for s in range(max(n_slots, len(copies))):
        if s < len(copies):
            for copy in copies[s]:
                copy.start()
        if s < n_slots:
            end_part, mid_part = part_of(of_end[s], leads[s], k_count), part_of(of_mid[s], leads[n_slots + s], k_count)
            m_copies(flags, turns, end_part, mid_part, m_buf.at[s], m_sems.at[s])
    keep_flags(flags, flags_out)

    def out_copy(t):
        start = pl.multiple_of(t * step, STEP)
        target = left.at[:, :, :, pl.ds(start, step)]
        return pltpu.make_async_copy(out_buf.at[t % 2], target, out_sems.at[t % 2])

    def one_step(t, carry):
        @pl.when(t >= 2)
        def _():
            out_copy(t - 2).wait()

        for copy in w_copies(w_refs[0], places[0], turns, w_buf, 0, 0, step, w_sems.at[t]):
            copy.wait()
        @pl.when(t == 0)
        def _():
            for s in range(n_slots):
                pltpu.make_async_copy(m_buf.at[s], m_buf.at[s], m_sems.at[s]).wait()

        for at in range(0, step, STEP):
            start = pl.multiple_of(t * step + at, STEP)
            for s in range(n_slots):
                lhs = m_buf[s].reshape(k_count * both, depth)
                w_re, w_im = w_buf[0, :, pl.ds(start, STEP)], w_buf[1, :, pl.ds(start, STEP)]
                out_buf[t % 2, s, :, :, at : at + STEP] = left_tile(lhs, w_re, w_im, k_count, both)
        out_copy(t).start()
        return carry

    lax.fori_loop(0, total, one_step, 0)
    for t in range(max(total - 2, 0), total):
        out_copy(t).wait()


def first_product(flags, chunks, turns, first_slot, n_slots, of_end, of_mid):
    depth = len(turns) * chunks[0][2][0].shape[0]
    both, k_count = of_end[first_slot][0].shape[1], 4
    columns = tuple((first, width) for first, width, _, _ in chunks)
    span = sum(width for _, width in columns)
    slots = range(first_slot, first_slot + n_slots)
    step = WIDE_STEP if n_slots == 1 and all(width % WIDE_STEP == 0 for _, width in columns) else STEP
    chosen = [of_end[s] for s in slots] + [of_mid[s] for s in slots]
    operands = [ref for _, _, blocks, _ in chunks for ref in blocks] + [ref for ref, _ in chosen]
    return pl.pallas_call(
        functools.partial(
            first_kernel,
            first_slot=first_slot,
            n_slots=n_slots,
            columns=columns,
            places=tuple(places for _, _, _, places in chunks),
            leads=tuple(lead for _, lead in chosen),
            turns=turns,
            step=step,
        ),
        out_shape=(jax.ShapeDtypeStruct((n_slots, k_count, both, span), jnp.float32), FLAGS),
        in_specs=[IN_SMEM] + [ANYWHERE] * len(operands),
        out_specs=(ANYWHERE, IN_SMEM),
        scratch_shapes=[
            pltpu.VMEM((2, depth, span), jnp.bfloat16),
            pltpu.VMEM((n_slots, k_count, both, depth), jnp.bfloat16),
            pltpu.VMEM((2, n_slots, k_count, both, step), jnp.float32),
            pltpu.SemaphoreType.DMA((span // step, 8)),
            pltpu.SemaphoreType.DMA((n_slots,)),
            pltpu.SemaphoreType.DMA((2,)),
        ],
        compiler_params=PARAMS,
        cost_estimate=COST,
        name="first_product",
    )(flags, *operands)


def stored_kernel(flags, *refs, n_slots, n_lefts, columns, places, leads):
    first, width = columns
    w_refs, of_end, of_mid = refs[:5], refs[5 : 5 + n_slots], refs[5 + n_slots : 5 + 2 * n_slots]
    matched, rest = refs[5 + 2 * n_slots : 13 + 2 * n_slots], refs[13 + 2 * n_slots :]
    lefts, (sums, flags_out, w_buf, m_buf, c_buf, left_buf, w_sems, m_sems, c_sems, left_sems) = rest[:n_lefts], rest[n_lefts:]
    depth = w_buf.shape[1]
    all_slots, k_count, both, _ = c_buf.shape
    sources = [left.at[i] for left in lefts for i in range(left.shape[0])]
    wide = WIDE_STEP if width % WIDE_STEP == 0 else STEP
    n_steps = width // wide

    def w_loads(i):
        return w_copies(w_refs, places, (3,), w_buf, i * wide, i * wide, wide, w_sems.at[i])

    def left_load(source, s, i):
        span = slice(i * wide, (i + 1) * wide)
        return pltpu.make_async_copy(source.at[:, :, span], left_buf.at[s, :, :, span], left_sems.at[s, i])

    for s in range(all_slots):
        if s < n_slots:
            end_part, mid_part = part_of(of_end[s], leads[s], k_count), part_of(of_mid[s], leads[n_slots + s], k_count)
            m_copies(flags, (3,), end_part, mid_part, m_buf.at[s], m_sems.at[s])
        for i in range(n_steps):
            if s == 0:
                for copy in w_loads(i):
                    copy.start()
            left_load(sources[s], s, i).start()
        matched_copies(flags, matched, leads[2 * n_slots :], c_buf, (s,), first, width, c_sems)
    keep_flags(flags, flags_out)

    def second(s):
        matched_wait(c_buf, s, c_sems)
        for k in range(k_count):
            sums[s, k] = times_matched(left_buf[s, k], c_buf[s, (k + flags[3]) % k_count])

    def left_wait(s, i):
        some = left_buf.at[s, :, :, :wide]
        pltpu.make_async_copy(some, some, left_sems.at[s, i]).wait()

    def one_step(t, carry):
        s, step = t // n_steps, t % n_steps
        left_wait(s, step)

        @pl.when(step == 0)
        def _():
            pltpu.make_async_copy(m_buf.at[s], m_buf.at[s], m_sems.at[s]).wait()

        @pl.when(s == 0)
        def _():
            for copy in w_copies(w_refs, places, (3,), w_buf, 0, 0, wide, w_sems.at[step]):
                copy.wait()

        lhs = m_buf[s].reshape(k_count * both, depth)
        for at in range(0, wide, STEP):
            start = pl.multiple_of(step * wide + at, STEP)
            tile = left_tile(lhs, w_buf[0, :, pl.ds(start, STEP)], w_buf[1, :, pl.ds(start, STEP)], k_count, both)
            left_buf[s, :, :, pl.ds(start, STEP)] = left_buf[s, :, :, pl.ds(start, STEP)] + tile

        @pl.when(step == n_steps - 1)
        def _():
            second(s)

        return carry

    lax.fori_loop(0, n_slots * n_steps, one_step, 0)

    def only_second(s, carry):
        for i in range(n_steps):
            left_wait(s, i)
        second(s)
        return carry

    lax.fori_loop(n_slots, all_slots, only_second, 0)


def stored_products(flags, chunk, of_end, of_mid, matched, lefts):
    n_slots, k_count, both, _ = lefts[0].shape
    all_slots = sum(left.shape[0] for left in lefts)
    first, width, blocks, places = chunk
    rows = blocks[0].shape[0]
    chosen = list(of_end[:n_slots]) + list(of_mid[:n_slots]) + list(matched)
    operands = list(blocks) + [ref for ref, _ in chosen] + list(lefts)
    return pl.pallas_call(
        functools.partial(
            stored_kernel,
            n_slots=n_slots,
            n_lefts=len(lefts),
            columns=(first, width),
            places=places,
            leads=tuple(lead for _, lead in chosen),
        ),
        out_shape=(jax.ShapeDtypeStruct((all_slots, k_count, both, both), jnp.float32), FLAGS),
        in_specs=[IN_SMEM] + [ANYWHERE] * len(operands),
        out_specs=(IN_VMEM, IN_SMEM),
        scratch_shapes=[
            pltpu.VMEM((2, rows, width), jnp.bfloat16),
            pltpu.VMEM((n_slots, k_count, both, rows), jnp.bfloat16),
            pltpu.VMEM((all_slots, k_count, both, width), jnp.bfloat16),
            pltpu.VMEM((all_slots, k_count, both, width), jnp.float32),
            pltpu.SemaphoreType.DMA((width // STEP, 2)),
            pltpu.SemaphoreType.DMA((n_slots,)),
            pltpu.SemaphoreType.DMA((all_slots,)),
            pltpu.SemaphoreType.DMA((all_slots, width // STEP)),
        ],
        compiler_params=PARAMS,
        cost_estimate=COST,
        name="stored_products",
    )(flags, *operands)


def both_kernel(flags, *refs, n_slots, columns, places, leads):
    n_chunks = len(columns)
    first = columns[0][0]
    w_refs, rest = [refs[5 * i : 5 * i + 5] for i in range(n_chunks)], refs[5 * n_chunks :]
    of_end, of_mid, rest = rest[:n_slots], rest[n_slots : 2 * n_slots], rest[2 * n_slots :]
    matched, sums_in, kept, given = rest[:8], rest[8], rest[9], rest[10]
    w_buf, m_buf, c_buf, left_buf, acc, w_sems, m_sems, c_sems, sums_sem = rest[11:]
    depth, span = w_buf.shape[1:]
    _, k_count, both, _ = m_buf.shape
    n_tiles = span // STEP
    turns = (0, 1, 2, 3)

    tiles = [(i, at) for i in range(n_chunks) for at in range(0, columns[i][1], STEP)]

    def w_tile(number):
        i, at = tiles[number]
        return w_copies(w_refs[i], places[i], turns, w_buf, at, number * STEP, STEP, w_sems.at[number])

    def m_start(s):
        end_part, mid_part = part_of(of_end[s], leads[s], k_count), part_of(of_mid[s], leads[n_slots + s], k_count)
        m_copies(flags, turns, end_part, mid_part, m_buf.at[s], m_sems.at[s])

    def c_start(s):
        matched_copies(flags, matched, leads[2 * n_slots :], c_buf, (s,), first, span, c_sems)

    for copy in w_tile(0):
        copy.start()
    m_start(0)
    for i in range(1, n_tiles):
        for copy in w_tile(i):
            copy.start()
    m_start(1)
    c_start(0)
    sums_copy = pltpu.make_async_copy(sums_in, acc, sums_sem)
    sums_copy.start()

    wide = WIDE_STEP if span % WIDE_STEP == 0 else STEP
    n_steps = span // wide

    def one_step(t, carry):
        s, step = t // n_steps, t % n_steps

        @pl.when(s == 0)
        def _():
            for i in range(wide // STEP):
                number = step * (wide // STEP) + i
                for copy in w_copies(w_refs[0], places[0], turns, w_buf, 0, 0, STEP, w_sems.at[number]):
                    copy.wait()

        @pl.when(step == 0)
        def _():
            pltpu.make_async_copy(m_buf.at[s], m_buf.at[s], m_sems.at[s]).wait()
            for j in range(n_slots - 1):
                @pl.when(s == j)
                def _():
                    if j + 2 < n_slots:
                        m_start(j + 2)
                    c_start(j + 1)

        lhs = m_buf[s].reshape(k_count * both, depth)
        for at in range(0, wide, STEP):
            start = pl.multiple_of(step * wide + at, STEP)
            tile = left_tile(lhs, w_buf[0, :, pl.ds(start, STEP)], w_buf[1, :, pl.ds(start, STEP)], k_count, both)
            left_buf[:, :, pl.ds(start, STEP)] = tile

        @pl.when(step == n_steps - 1)
        def _():
            @pl.when(s == 0)
            def _():
                sums_copy.wait()

            matched_wait(c_buf, s, c_sems)
            for k in range(k_count):
                acc[s, k] = acc[s, k] + times_matched(left_buf[k], c_buf[s, (k + flags[3]) % k_count])

        return carry

    lax.fori_loop(0, n_slots * n_steps, one_step, 0)
    pairs, own_k = both // 2, k_count // 2
    for s in range(n_slots):
        above = jnp.where(flags[2] == 0, s, (n_slots - s) % n_slots)
        for k in range(k_count):
            terms = acc[s, k]
            real_part = terms[:pairs, :pairs] - terms[pairs:, pairs:]
            imaginary_part = terms[:pairs, pairs:] + terms[pairs:, :pairs]
            block = jnp.concatenate([real_part, imaginary_part], axis=1)

            @pl.when(flags[5] == k // own_k)
            def _():
                kept[above, k % own_k] = block

            @pl.when(flags[5] != k // own_k)
            def _():
                given[above, k % own_k] = block


def both_products(flags, chunks, of_end, of_mid, matched, sums):
    n_slots, k_count, both, _ = sums.shape
    depth = 4 * chunks[0][2][0].shape[0]
    columns = tuple((first, width) for first, width, _, _ in chunks)
    span = sum(width for _, width in columns)
    chosen = list(of_end) + list(of_mid) + list(matched)
    operands = [ref for _, _, blocks, _ in chunks for ref in blocks] + [ref for ref, _ in chosen] + [sums]
    halves = jax.ShapeDtypeStruct((n_slots, k_count // 2, both // 2, both), jnp.float32)
    return pl.pallas_call(
        functools.partial(
            both_kernel,
            n_slots=n_slots,
            columns=columns,
            places=tuple(places for _, _, _, places in chunks),
            leads=tuple(lead for _, lead in chosen),
        ),
        out_shape=(halves, halves),
        in_specs=[IN_SMEM] + [ANYWHERE] * len(operands),
        out_specs=(IN_VMEM, IN_VMEM),
        scratch_shapes=[
            pltpu.VMEM((2, depth, span), jnp.bfloat16),
            pltpu.VMEM((n_slots, k_count, both, depth), jnp.bfloat16),
            pltpu.VMEM((n_slots, k_count, both, span), jnp.bfloat16),
            pltpu.VMEM((k_count, both, span), jnp.float32),
            pltpu.VMEM((n_slots, k_count, both, both), jnp.float32),
            pltpu.SemaphoreType.DMA((span // STEP, 8)),
            pltpu.SemaphoreType.DMA((n_slots,)),
            pltpu.SemaphoreType.DMA((n_slots,)),
            pltpu.SemaphoreType.DMA,
        ],
        compiler_params=PARAMS,
        cost_estimate=COST,
        name="both_products",
    )(flags, *operands)


def turn_kernel(flags, first, second, first_turned, second_turned, turned_pair):
    first_turned[0] = first[0].T
    second_turned[0] = second[0].T
    turned_pair[0, 0] = second_turned[0]
    turned_pair[1, 0] = first_turned[0]


def turned_parts(flags, densities):
    k_count, n_rows, both = densities.shape
    quarter = n_rows // 4

    def part(which):
        return pl.BlockSpec((1, quarter, both), lambda k, flags: (k, flags[which], 0))

    one = pl.BlockSpec((1, both, quarter), lambda k, flags: (k, 0, 0))
    first, second, both_parts = pl.pallas_call(
        turn_kernel,
        out_shape=(
            jax.ShapeDtypeStruct((k_count, both, quarter), densities.dtype),
            jax.ShapeDtypeStruct((k_count, both, quarter), densities.dtype),
            jax.ShapeDtypeStruct((2, k_count, both, quarter), densities.dtype),
        ),
        grid_spec=pltpu.PrefetchScalarGridSpec(
            num_scalar_prefetch=1,
            grid=(k_count,),
            in_specs=[part(6), part(7)],
            out_specs=[
                one,
                one,
                pl.BlockSpec((2, 1, both, quarter), lambda k, flags: (0, k, 0, 0)),
            ],
        ),
        compiler_params=PARAMS,
        cost_estimate=COST,
        name="turned_parts",
    )(flags, densities, densities)
    return first, second, both_parts.reshape(2 * k_count, both, quarter)


def body(densities, screened, partner, pair_order):
    k_count, n_rows, both = densities.shape
    pair_count = both // 2
    quarter = n_rows // 4
    panel = screened.shape[2]
    widths = (panel // 2, panel // 4, panel // 4)
    firsts = [sum(widths[:n]) for n in range(3)]
    k_owner = lax.axis_index("ka")
    c = lax.axis_index("ga")
    z, b = k_owner // 4, k_owner % 4
    half, odd = z // 2, z % 2
    offset = partner[0] % k_count
    ends = (z == 0) | (z == 3)
    flags = jnp.stack([b, c == odd, half, offset, ends, c, 2 * (1 - odd) + c, 2 * odd + c]).astype(jnp.int32)
    rows = screened.shape[1]

    part = (k_count, both, quarter)

    def own_pieces(n, when, at=0):
        first, width = firsts[n], widths[n]
        return [
            (when, screened, real(first, width), columns_of(at, width)),
            (when, screened, imaginary(first, width), columns_of(at + width, width)),
        ]

    def far_part(*numbers):
        pieces, at = [], 0
        for n in numbers:
            pieces += own_pieces(n, own_far, at)
            at += 2 * widths[n]
        return (rows, at), pieces

    def sent_far(value):
        return moved(value, lambda z, b, c: (z ^ 1, b, 1 - c) if c != z % 2 else None)

    def panel_parts(n, arrived, at=0, before=None):
        copies = 0 if before is None else 1
        pieces = [piece + (copies,) for piece in own_pieces(n, own_near)]
        pieces.append((own_far, arrived, columns_of(at, 2 * widths[n]), columns_of(0, 2 * widths[n]), copies))
        if before is None:
            return (((rows, 2 * widths[n]), pieces),)
        x_side, y_side = before
        passed = widths[n - 1]
        shape, place = (rows, 2 * widths[n] + passed), columns_of(2 * widths[n], passed)
        return (
            (shape, pieces + [(always, y_side, columns_of(passed, passed), place)]),
            (shape, [(always, x_side, columns_of(0, passed), place)]),
        )

    first_part, second_part = slots_from(0, k_count), slots_from(k_count, k_count)

    flags, sent_0 = moves(flags, (), far_part(0))
    arrived_0 = sent_far(sent_0)
    own_first, own_second, own_both = turned_parts(flags, densities)
    swapped_0 = other_core(own_second)
    pair_a, mid_ad = end_with_mid(own_first), mid_with_mid(own_both)

    flags, sent_1, sent_2 = moves(flags, (own_first,), far_part(1), far_part(2))

    flags, panel_0 = moves(flags, (swapped_0,), *panel_parts(0, arrived_0))
    arrived_1 = sent_far(sent_1)
    x_0, y_0 = along_x(panel_0), along_y(panel_0)

    flags, to_pair, to_mid = moves(
        flags,
        (),
        (part, [(at_end, own_second, whole, whole), (at_mid, mid_ad, first_part, whole)]),
        (part, [(always, pair_a, whole, whole)]),
    )
    pair_b, mid_b = end_with_mid(to_pair), mid_with_mid(to_mid)

    flags, to_x, to_y, sent_2 = moves(flags, (), *panel_parts(1, arrived_1, 0, (x_0, y_0)), passing=(sent_2,))
    x_1, y_1 = along_x(to_x), along_y(to_y)
    panel_1 = to_x
    arrived_2 = sent_far(sent_2)

    chunk_0 = (firsts[0], widths[0], (panel_0, x_0, y_0, y_0, x_0), (widths[0], 0, 0))
    early_end, early_mid = [(own_second, 0), (pair_a, 0)], [(own_first, 0), (mid_ad, 0)]
    left_0, flags = first_product(flags, [chunk_0], (0, 1, 2), 0, 2, early_end, early_mid)

    flags, pair_b, mid_b = moves(flags, (arrived_2,), passing=(pair_b, mid_b))
    swapped_a = other_core(pair_a)
    pair_c, mid_c = mid_to_end(mid_b), mid_with_mid(pair_b)
    of_end = [(own_second, 0), (pair_a, 0), (pair_b, 0), None]
    of_mid = [(own_first, 0), (mid_ad, 0), (mid_b, 0), (pair_b, 0)]
    every = (0, 1, 2, 3)

    flags, to_x, to_y = moves(flags, (), *panel_parts(2, arrived_2, 0, (x_1, y_1)))
    x_2, y_2 = along_x(to_x), along_y(to_y)
    panel_2 = to_x
    chunk_0 = (firsts[0], widths[0], (panel_0, x_0, y_0, y_1, x_1), (widths[0], 2 * widths[1], 2 * widths[1]))
    left_2, flags = first_product(flags, [chunk_0], every, 2, 1, of_end, of_mid)

    late_pieces = [(at_end, pair_b, whole, whole), (at_mid, mid_ad, second_part, whole)]
    flags, late_1 = moves(flags, (), (part, late_pieces))
    flags, late_2, late_1 = moves(
        flags, (swapped_a,), (part, [(at_end, pair_c, whole, whole), (at_mid, mid_c, whole, whole)]), passing=(late_1,)
    )
    swapped_1, swapped_2 = other_core(late_1), other_core(late_2)
    of_end[3] = (pair_c, 0)
    matched = [(own_second, 0), (swapped_0, 0), (pair_a, 0), (swapped_a, 0)]
    matched += [(late_1, 0), (swapped_1, 0), (late_2, 0), (swapped_2, 0)]
    left_3, flags = first_product(flags, [chunk_0], every, 3, 1, of_end, of_mid)

    shape = (rows, widths[2])
    flags, to_x, to_y = moves(
        flags,
        (),
        (shape, [(always, y_2, columns_of(widths[2], widths[2]), whole)]),
        (shape, [(always, x_2, columns_of(0, widths[2]), whole)]),
    )
    x_3, y_3 = along_x(to_x), along_y(to_y)
    chunk_1 = (firsts[1], widths[1], (panel_1, x_1, y_1, y_2, x_2), (widths[1], 2 * widths[2], 2 * widths[2]))
    sums_0, flags = stored_products(flags, chunk_0, of_end, of_mid, matched, [left_0, left_2, left_3])
    chunk_2 = (firsts[2], widths[2], (panel_2, x_2, y_2, y_3, x_3), (widths[2], 0, 0))
    mine, given = both_products(flags, [chunk_1, chunk_2], of_end, of_mid, matched, sums_0)

    mine = mine + other_core(given)
    total = jnp.stack([mine[0], mine[3]])
    for shift in (1, 2, 3):
        sent = jnp.stack([mine[shift], mine[shift - 1]])
        total = total + moved(sent, lambda z, b, c: ((z + shift) % 4, b, c))
    theirs = other_core(total)
    total = jnp.where(c == 0, jnp.concatenate([total, theirs], axis=1), jnp.concatenate([theirs, total], axis=1))
    total = total.reshape(2 * k_count, pair_count, both)
    order_table = (jnp.arange(pair_count)[:, None] == pair_order[None, :]).astype(jnp.float32)
    filed = reorder(total[:, :, :pair_count], total[:, :, pair_count:], order_table)
    sources = (jnp.arange(k_count) - offset) % k_count
    mirror = conjugate_side(jnp.take(filed[k_count:], sources, axis=0), pair_count)
    return (filed[:k_count], mirror)


def solution(mesh):
    in_specs = (P("ka", None, None), P(None, "ka", "ga"), P(), P())
    out_specs = (P("ka", None, None), P("ka", None, None))
    planes = mesh.shape["ka"] == 16 and mesh.shape["ga"] == 2
    chosen = body if planes else general_body
    return jax.shard_map(chosen, mesh=mesh, in_specs=in_specs, out_specs=out_specs, check_vma=False)
```
